512 devices in a mesh: seq: 16 (over z), chan: 32 (over x, y, core).
Axes of the slice: x: 4, y: 4, z: 16, core: 2. Of those that a mesh axis runs over, the one named last changes fastest.
Arguments:
- features: bfloat16 [3, 128, 131072], P(None, 'chan', 'seq'), may hold values from -6 to 6
- short_taps: float32 [3, 128, 3], P(None, 'chan'), may hold values from -3 to 3
- long_filter: float32 [128, 131072], P('chan', 'seq'), may hold values from -2 to 2
- skip_gain: float32 [128], P('chan'), may hold values from 0.5 to 1.5
- out_weight: bfloat16 [128, 4096], P(None, 'chan'), may hold values from -0.5 to 0.5
Outputs:
- projected: bfloat16 [131072, 4096], P('seq', 'chan')
The draws below stay inside these ranges and needn't reach their ends.
All inputs are finite; a program needn't handle non-finite values.
Results may differ from the reference program's by a relative error of at most 0.0049.
Values may be sent and summed in bfloat16 or wider, within the bound.
No kernel may reach another device: no remote copies, remote signals or barrier semaphores. Data moves between devices by JAX's collectives and lax.ppermute only.
A program may use at most 64 MiB of HBM per device.

```python
import math
import jax
import jax.numpy as jnp
from jax import lax

D = 4096
SLAB_CHANNELS = 128
SEQUENCE_TOKENS = 131072


def draw_long_filter(key, part):
    key = jax.random.fold_in(key, 11)
    key_kind, key_fast, key_slow, random_key_position, random_key_removal, key_rough = jax.random.split(key, 6)
    fast_cut = 5
    is_fast = jax.random.randint(key_kind, (SLAB_CHANNELS,), 0, 10) < fast_cut
    fast_rate = 2.0 / jax.random.uniform(key_fast, (SLAB_CHANNELS,), jnp.float32, 30.0, 50.0)
    slow_rate = jnp.exp(jax.random.uniform(key_slow, (SLAB_CHANNELS,), jnp.float32, math.log(0.05), math.log(0.9))) / SEQUENCE_TOKENS
    decay_rate = jnp.where(is_fast, fast_rate, slow_rate)
    positions = jnp.arange(SEQUENCE_TOKENS, dtype=jnp.float32)
    decay_profile = jnp.exp(-decay_rate[:, None] * positions[None, :])
    spike_position = jax.random.randint(random_key_position, (SLAB_CHANNELS, 2), 0, SEQUENCE_TOKENS)
    spike_removed = jax.random.uniform(random_key_removal, (SLAB_CHANNELS, 2), jnp.float32, 0.2, 0.5)
    token_position_index = jnp.arange(SEQUENCE_TOKENS, dtype=jnp.int32)
    for spike_index in range(2):
        check_result = token_position_index[None, :] >= spike_position[:, spike_index:spike_index + 1]
        decay_profile = decay_profile * jnp.where(check_result, 1.0 - spike_removed[:, spike_index:spike_index + 1], 1.0)
    amplitude = jnp.sqrt(jnp.expm1(-2.0 * decay_rate) / jnp.expm1(-2.0 * decay_rate * SEQUENCE_TOKENS))
    rough_part = jnp.clip(jax.random.normal(key_rough, (SLAB_CHANNELS, SEQUENCE_TOKENS), jnp.float32), -4.0, 4.0)
    return amplitude[:, None] * decay_profile * rough_part


def steps_of(stream_key, shape, pieces, smallest, high):
    def one(position, blocks):
        steps = jax.random.uniform(jax.random.fold_in(jax.random.fold_in(stream_key, 6), position), (blocks,), jnp.float32, smallest / len(pieces), high / len(pieces))
        return jnp.repeat(jnp.exp(steps), shape[position] // blocks).reshape((-1,) + (1,) * (len(shape) - position - 1))

    factor_of = one(*pieces[0])
    for cut in pieces[1:]:
        factor_of = factor_of * one(*cut)
    return factor_of


def normal_values(rng, shape, spread, most, cuts=(), kind=jnp.bfloat16):
    values = spread * jax.random.normal(rng, shape, jnp.float32)
    if cuts:
        values = values * steps_of(rng, shape, cuts, -0.22, 0.18)
    return jnp.clip(values, -most, most).astype(kind)


def setup_inputs(seed: int = 0) -> dict:
    seeds = jax.random.split(jax.random.key(seed), 6)
    features = normal_values(seeds[0], (3, SLAB_CHANNELS, SEQUENCE_TOKENS), 1.0, 6.0, ((1, 32), (2, 16)))
    short_taps = normal_values(seeds[1], (3, SLAB_CHANNELS, 3), 0.6, 3.0, ((1, 32),), jnp.float32)
    long_filter = draw_long_filter(jax.random.fold_in(seeds[5], 71), 0)
    skip_gain = jnp.clip(0.5 + 1.0 * jax.random.uniform(seeds[3], (SLAB_CHANNELS,), jnp.float32) ** steps_of(seeds[3], (SLAB_CHANNELS,), ((0, 32),), -0.2, 0.2), 0.5, 1.5)
    out_weight = normal_values(seeds[4], (SLAB_CHANNELS, D), SLAB_CHANNELS ** -0.5, 0.5, ((1, 32),))
    return {"features": features, "short_taps": short_taps, "long_filter": long_filter, "skip_gain": skip_gain, "out_weight": out_weight}


def reference(features, short_taps, long_filter, skip_gain, out_weight):
    length = features.shape[-1]
    padded = jnp.pad(features, ((0, 0), (0, 0), (2, 0)))
    short_mixed = short_taps[:, :, 0:1] * padded[:, :, 2:2 + length]
    short_mixed = short_mixed + short_taps[:, :, 1:2] * padded[:, :, 1:1 + length]
    short_mixed = short_mixed + short_taps[:, :, 2:3] * padded[:, :, 0:length]
    queries = short_mixed[0]
    product = short_mixed[1] * short_mixed[2]
    spectrum = jnp.fft.rfft(product, n=2 * length) * jnp.fft.rfft(long_filter, n=2 * length)
    convolved = jnp.fft.irfft(spectrum, n=2 * length)[:, :length]
    gated_rows = (queries * (convolved + skip_gain[:, None] * product)).astype(jnp.bfloat16)
    block_len = math.gcd(length, 8192)
    block_count = length // block_len
    blocks = gated_rows.reshape(gated_rows.shape[0], block_count, block_len).transpose(1, 0, 2)

    def project_block(block_rows):
        result = lax.dot_general(block_rows, out_weight, (((0,), (0,)), ((), ())), preferred_element_type=jnp.float32)
        return result.astype(jnp.bfloat16)

    projected = lax.map(project_block, blocks)
    return projected.reshape(length, out_weight.shape[1])
```

```python
import math

import jax
import jax.numpy as jnp
import ml_dtypes
import numpy as np
from jax import lax
from jax.experimental import pallas as pl
from jax.experimental.pallas import tpu as pltpu
from jax.sharding import PartitionSpec as P

N1, N2 = 64, 128
BLOCK = N1 * N2
SLICES = 16
f32, bf16 = jnp.float32, jnp.bfloat16


def split_table(table):
    high = table.astype(ml_dtypes.bfloat16)
    low = (table - high.astype(np.float64)).astype(ml_dtypes.bfloat16)
    return high, low


def tables():
    row = np.arange(2 * N1)
    k1 = 4 * (row // 8) + row % 4
    imag = (row // 4) % 2 == 1
    n1, n2 = np.arange(N1), np.arange(N2)
    phase = 2 * math.pi * np.outer(k1 + 0.25, n1) / N1
    outer = np.where(imag[:, None], -np.sin(phase), np.cos(phase))
    oh, ol = split_table(outer)
    forward_outer = np.concatenate([oh, oh, ol], axis=1)
    ih, il = split_table(outer.T / BLOCK)
    inverse_outer = np.concatenate([ih, ih, il], axis=1)
    angle = 2 * math.pi * np.outer(k1 + 0.25, n2) / BLOCK
    turn_cos = np.cos(angle).astype(np.float32)
    turn_sin = np.where(imag[:, None], -np.sin(angle), np.sin(angle)).astype(np.float32)
    phase = 2 * math.pi * np.outer(n2, n2) / N2

    def inner(sign):
        high, low = split_table(np.concatenate([np.cos(phase), sign * np.sin(phase)], axis=1))
        return np.concatenate([high, high, low], axis=0)

    return forward_outer, inverse_outer, turn_cos, turn_sin, inner(-1.0), inner(1.0)


def halves_swapped(tile):
    rows = tile.shape[0]
    return pltpu.roll(tile.reshape(rows // 8, 8, N2), 4, 1).reshape(rows, N2)


def split(value):
    high = value.astype(bf16)
    return high, (value - high.astype(f32)).astype(bf16)


def imag_sign(rows):
    return jnp.where(lax.broadcasted_iota(jnp.int32, (rows, N2), 0) % 8 < 4, -1.0, 1.0).astype(f32)


def inner_stage(rows, table):
    high, low = split(rows)
    both = jnp.dot(jnp.concatenate([high, low, high], axis=1), table, preferred_element_type=f32)
    return both[:, :N2] + imag_sign(rows.shape[0]) * halves_swapped(both[:, N2:])


def short_filter(stream, edge, taps_ref, at):
    row = lax.broadcasted_iota(jnp.int32, (N1, N2), 0)
    lane = lax.broadcasted_iota(jnp.int32, (N1, N2), 1)
    total = taps_ref[3 * at] * stream
    edge = jnp.broadcast_to(edge, (8, N2))
    for lag in (1, 2):
        turned = pltpu.roll(stream, lag, 1)
        before = pltpu.roll(turned, 1, 0)
        first = jnp.concatenate([pltpu.roll(edge, lag, 1)] + [before[8:]], axis=0)
        before = jnp.where(row == 0, first, before)
        total = total + taps_ref[3 * at + lag] * jnp.where(lane < lag, before, turned)
    return total


def forward_kernel(feat_ref, edge_ref, taps_ref, filt_ref, outer_ref, cos_ref, sin_ref, inner_ref, out_ref):
    signals = []
    for c in range(4):
        mixed = [
            short_filter(feat_ref[i, c].astype(f32), edge_ref[4 * i + c : 4 * i + c + 1].astype(f32), taps_ref, 4 * i + c)
            for i in (1, 2)
        ]
        signals.append(mixed[0] * mixed[1])
    signals += [filt_ref[c] for c in range(4)]
    high, low = split(jnp.concatenate(signals, axis=1))
    stacked = jnp.concatenate([high, low, high], axis=0)
    first = jnp.dot(outer_ref[...], stacked, preferred_element_type=f32)
    for pair in range(4):
        done = []
        for s in (2 * pair, 2 * pair + 1):
            tile = first[:, N2 * s : N2 * (s + 1)]
            tile = tile * cos_ref[...] + halves_swapped(tile) * sin_ref[...]
            done.append(inner_stage(tile, inner_ref[...]).reshape(SLICES, 8, N2))
        out_ref[:, 16 * pair : 16 * pair + 16, :] = jnp.concatenate(done, axis=1).astype(bf16)


def gate_kernel(feat_ref, edge_ref, taps_ref, gain_ref, queries_ref, direct_ref):
    for c in range(4):
        mixed = [
            short_filter(feat_ref[i, c].astype(f32), edge_ref[4 * i + c : 4 * i + c + 1].astype(f32), taps_ref, 4 * i + c)
            for i in range(3)
        ]
        queries_ref[c] = mixed[0]
        direct_ref[c] = gain_ref[c] * (mixed[1] * mixed[2])


def mix_kernel(in_ref, out_ref):
    top = lax.broadcasted_iota(jnp.int32, (8, N2), 0) < 4
    for pair in range(2):
        sums = []
        for side in range(2):
            data, filt = [], []
            for block in range(SLICES):
                both = in_ref[block, 16 * pair : 16 * pair + 16, :].astype(f32)
                data.append(both[8 * side : 8 * side + 8])
                both = in_ref[block, 32 + 16 * pair : 48 + 16 * pair, :].astype(f32)
                filt.append(both[8 * side : 8 * side + 8])
            swapped = [pltpu.roll(tile, 4, 0) for tile in data]
            real_parts, imag_parts = [], []
            for m in range(SLICES):
                tile = filt[m]
                if m:
                    turned = pltpu.roll(filt[m - 1], 4, 0)
                    tile = tile + jnp.where(top, -turned, turned)
                turned = pltpu.roll(tile, 4, 0)
                real_parts.append(jnp.where(top, tile, turned))
                imag_parts.append(jnp.where(top, -turned, tile))
            row = []
            for d in range(SLICES):
                total = None
                for e in range(d + 1):
                    term = data[e] * real_parts[d - e] + swapped[e] * imag_parts[d - e]
                    total = term if total is None else total + term
                row.append(total)
            sums.append(row)
        for d in range(SLICES):
            out_ref[d, 16 * pair : 16 * pair + 16, :] = jnp.concatenate([sums[0][d], sums[1][d]], axis=0).astype(bf16)


def inverse_kernel(in_ref, queries_ref, direct_ref, outer_ref, cos_ref, sin_ref, inner_ref, out_ref):
    turned = []
    for pair in range(2):
        both = in_ref[:, 16 * pair : 16 * pair + 16, :].astype(f32)
        for side in range(2):
            tile = both[:, 8 * side : 8 * side + 8, :].reshape(2 * N1, N2)
            tile = inner_stage(tile, inner_ref[...])
            turned.append(tile * cos_ref[...] - halves_swapped(tile) * sin_ref[...])
    high, low = split(jnp.concatenate(turned, axis=1))
    stacked = jnp.concatenate([high, low, high], axis=0)
    convolved = jnp.dot(outer_ref[...], stacked, preferred_element_type=f32)
    for c in range(4):
        gated = queries_ref[c] * (convolved[:, N2 * c : N2 * (c + 1)] + direct_ref[c])
        gated = gated.astype(bf16)
        for copy in range(out_ref.shape[0]):
            out_ref[copy, N1 * c : N1 * (c + 1), :] = gated


vmem = pl.BlockSpec(memory_space=pltpu.VMEM)
smem = pl.BlockSpec(memory_space=pltpu.SMEM)


def call(kernel, specs, shape, dtype, *operands):
    if isinstance(shape, list):
        out_shape, out_specs = [jax.ShapeDtypeStruct(s, dtype) for s in shape], [vmem] * len(shape)
    else:
        out_shape, out_specs = jax.ShapeDtypeStruct(shape, dtype), vmem
    return pl.pallas_call(
        kernel,
        out_shape=out_shape,
        in_specs=specs,
        out_specs=out_specs,
        compiler_params=pltpu.CompilerParams(vmem_limit_bytes=32 << 20),
        cost_estimate=pl.CostEstimate(flops=1 << 24, bytes_accessed=1 << 20, transcendentals=0),
    )(*operands)


def gated_copies(features, short_taps, long_filter, skip_gain, copies):
    forward_outer, inverse_outer, turn_cos, turn_sin, forward_inner, inverse_inner = map(jnp.asarray, tables())
    seq = lax.axis_size("seq")
    edge = features[:, :, BLOCK - N2 :].reshape(12, N2)
    edge = lax.ppermute(edge, "seq", [(z, z + 1) for z in range(seq - 1)])
    feat = features.reshape(3, 4, N1, N2)
    taps = short_taps.reshape(36)
    spectra = call(
        forward_kernel,
        [vmem, vmem, smem, vmem, vmem, vmem, vmem, vmem],
        (SLICES, 64, N2),
        bf16,
        feat,
        edge,
        taps,
        long_filter.reshape(4, N1, N2),
        forward_outer,
        turn_cos,
        turn_sin,
        forward_inner,
    )
    spectra = lax.all_to_all(spectra, "seq", 0, 0, tiled=True)
    queries, direct = call(
        gate_kernel, [vmem, vmem, smem, smem], [(4, N1, N2)] * 2, f32, feat, edge, taps, skip_gain
    )
    mixed = call(mix_kernel, [vmem], (SLICES, 32, N2), bf16, spectra)
    mixed = lax.all_to_all(mixed, "seq", 0, 0, tiled=True)
    return call(
        inverse_kernel,
        [vmem] * 7,
        (copies, 4 * N1, N2),
        bf16,
        mixed,
        queries,
        direct,
        inverse_outer,
        turn_cos,
        turn_sin,
        inverse_inner,
    )


def shards(features, short_taps, long_filter, skip_gain, out_weight):
    chan = lax.axis_size("chan")
    chips = chan // 2
    sent = gated_copies(features, short_taps, long_filter, skip_gain, chips)
    same_core = [[2 * chip + core for chip in range(chips)] for core in range(2)]
    own = lax.all_to_all(sent, "chan", 0, 0, tiled=True, axis_index_groups=same_core)
    other = lax.ppermute(own, "chan", [(d, d ^ 1) for d in range(chan)])
    core = lax.axis_index("chan") % 2
    weight = out_weight.reshape(chips, 2, 4, N2)
    own_weight = lax.dynamic_index_in_dim(weight, core, 1, False).reshape(4 * chips, N2)
    other_weight = lax.dynamic_index_in_dim(weight, 1 - core, 1, False).reshape(4 * chips, N2)
    rows = jnp.concatenate([own.reshape(4 * chips, BLOCK), other.reshape(4 * chips, BLOCK)], axis=0)
    weight = jnp.concatenate([own_weight, other_weight], axis=0)
    projected = lax.dot_general(rows, weight, (((0,), (0,)), ((), ())), preferred_element_type=f32)
    return projected.astype(bf16)


def solution(mesh):
    placed = (
        P(None, "chan", "seq"),
        P(None, "chan", None),
        P("chan", "seq"),
        P("chan"),
        P(None, "chan"),
    )
    return jax.shard_map(
        shards, mesh=mesh, in_specs=placed, out_specs=P("seq", "chan"), check_vma=False
    )
```

```python
import math

import jax
import jax.numpy as jnp
import ml_dtypes
import numpy as np
from jax import lax
from jax.experimental import pallas as pl
from jax.experimental.pallas import tpu as pltpu
from jax.sharding import PartitionSpec as P

N1, N2 = 64, 128
BLOCK = N1 * N2
SLICES = 16
f32, bf16 = jnp.float32, jnp.bfloat16


def split_table(table):
    high = table.astype(ml_dtypes.bfloat16)
    low = (table - high.astype(np.float64)).astype(ml_dtypes.bfloat16)
    return high, low


def tables():
    row = np.arange(2 * N1)
    k1 = 4 * (row // 8) + row % 4
    imag = (row // 4) % 2 == 1
    n1, n2 = np.arange(N1), np.arange(N2)
    phase = 2 * math.pi * np.outer(k1 + 0.25, n1) / N1
    outer = np.where(imag[:, None], -np.sin(phase), np.cos(phase))
    oh, ol = split_table(outer)
    forward_outer = np.concatenate([oh, oh, ol], axis=1)
    ih, il = split_table(outer.T / BLOCK)
    inverse_outer = np.concatenate([ih, ih, il], axis=1)
    angle = 2 * math.pi * np.outer(k1 + 0.25, n2) / BLOCK
    turn_cos = np.cos(angle).astype(np.float32)
    turn_sin = np.where(imag[:, None], -np.sin(angle), np.sin(angle)).astype(np.float32)
    phase = 2 * math.pi * np.outer(n2, n2) / N2

    def inner(sign):
        high, low = split_table(np.concatenate([np.cos(phase), sign * np.sin(phase)], axis=1))
        return np.concatenate([high, high, low], axis=0)

    return forward_outer, inverse_outer, turn_cos, turn_sin, inner(-1.0), inner(1.0)


def halves_swapped(tile):
    rows = tile.shape[0]
    return pltpu.roll(tile.reshape(rows // 8, 8, N2), 4, 1).reshape(rows, N2)


def split(value):
    high = value.astype(bf16)
    return high, (value - high.astype(f32)).astype(bf16)


def imag_sign(rows):
    return jnp.where(lax.broadcasted_iota(jnp.int32, (rows, N2), 0) % 8 < 4, -1.0, 1.0).astype(f32)


def inner_stage(rows, table):
    high, low = split(rows)
    both = jnp.dot(jnp.concatenate([high, low, high], axis=1), table, preferred_element_type=f32)
    return both[:, :N2] + imag_sign(rows.shape[0]) * halves_swapped(both[:, N2:])


def lane_index(shape):
    return lax.broadcasted_iota(jnp.int32, shape, 1)


def short_filter(stream, taps, edge=None):
    total = taps[:, 0:1] * stream
    for lag in (1, 2):
        turned = pltpu.roll(stream, lag, 1)
        head = turned[:, :N2]
        before = jnp.zeros_like(head) if edge is None else pltpu.roll(edge, lag, 1)
        head = jnp.where(lane_index(head.shape) < lag, before, head)
        total = total + taps[:, lag : lag + 1] * jnp.concatenate([head, turned[:, N2:]], axis=1)
    return total


def to_blocks(upper, lower, rows_ref):
    both = jnp.concatenate([upper, lower], axis=0)
    for n1 in range(N1):
        rows_ref[8 * n1 : 8 * n1 + 8, :] = both[:, N2 * n1 : N2 * (n1 + 1)]
    return [rows_ref[pl.ds(s, N1, stride=8), :] for s in range(8)]


def forward_kernel(
    feat_hbm, taps_hbm, filt_hbm, outer_hbm, cos_hbm, sin_hbm, inner_hbm, out_ref,
    feat_ref, taps_ref, filt_ref, outer_ref, cos_ref, sin_ref, inner_ref, rows_ref, sems,
):
    sources = (feat_hbm, taps_hbm, filt_hbm, outer_hbm, cos_hbm, sin_hbm, inner_hbm)
    places = (feat_ref, taps_ref, filt_ref, outer_ref, cos_ref, sin_ref, inner_ref)
    copies = [pltpu.make_async_copy(s, d, sems.at[n]) for n, (s, d) in enumerate(zip(sources, places))]
    for copy in copies:
        copy.start()
    for copy in copies[:2]:
        copy.wait()
    streams = [feat_ref[i].astype(f32) for i in range(3)]
    ends = [
        jnp.where(lane_index((4, N2)) < N1, stream[:, :N2], stream[:, BLOCK - N2 :]) for stream in streams
    ]
    ends = jnp.concatenate(ends + [jnp.zeros((4, N2), f32)], axis=0).astype(bf16)
    for device in range(SLICES):
        out_ref[device, 64:80, :] = ends
    product = short_filter(streams[1], taps_ref[1]) * short_filter(streams[2], taps_ref[2])
    copies[2].wait()
    signals = to_blocks(product, filt_ref[...], rows_ref)
    high, low = split(jnp.concatenate(signals, axis=1))
    stacked = jnp.concatenate([high, low, high], axis=0)
    for copy in copies[3:]:
        copy.wait()
    first = jnp.dot(outer_ref[...], stacked, preferred_element_type=f32)
    for pair in range(4):
        done = []
        for s in (2 * pair, 2 * pair + 1):
            tile = first[:, N2 * s : N2 * (s + 1)]
            tile = tile * cos_ref[...] + halves_swapped(tile) * sin_ref[...]
            done.append(inner_stage(tile, inner_ref[...]).reshape(SLICES, 8, N2))
        out_ref[:, 16 * pair : 16 * pair + 16, :] = jnp.concatenate(done, axis=1).astype(bf16)


def gate_kernel(
    feat_hbm, taps_hbm, spectra_hbm, gain_ref, queries_ref, direct_ref, feat_ref, taps_ref, ends_ref, rows_ref, sems
):
    device = lax.axis_index("seq")
    ends = spectra_hbm.at[jnp.maximum(device - 1, 0), pl.ds(64, 16), :]
    copies = [
        pltpu.make_async_copy(s, d, sems.at[n])
        for n, (s, d) in enumerate(((feat_hbm, feat_ref), (taps_hbm, taps_ref), (ends, ends_ref)))
    ]
    for copy in copies:
        copy.start()
    for copy in copies:
        copy.wait()
    edges = jnp.where(device > 0, ends_ref[...].astype(f32), 0.0)
    mixed = [
        short_filter(feat_ref[i].astype(f32), taps_ref[i], edges[4 * i : 4 * i + 4]) for i in range(3)
    ]
    rows = to_blocks(mixed[0], mixed[1] * mixed[2], rows_ref)
    for c in range(4):
        queries_ref[c] = rows[c]
        direct_ref[c] = gain_ref[c] * rows[4 + c]


def edge_terms(in_ref, taps_ref):
    lane = lane_index((16, N2))
    ends = [in_ref[block, 64:80, :].astype(f32) for block in range(SLICES)]
    taps = jnp.concatenate([taps_ref[0], taps_ref[1], taps_ref[2], taps_ref[2]], axis=0)
    taps = [jnp.broadcast_to(taps[:, k : k + 1], (16, N2)) for k in range(3)]

    def products(tokens):
        mixed = taps[2] * tokens + taps[1] * pltpu.roll(tokens, N2 - 1, 1) + taps[0] * pltpu.roll(tokens, N2 - 2, 1)
        return mixed * pltpu.roll(mixed, 12, 0)

    missing = [None]
    for block in range(1, SLICES):
        own = pltpu.roll(ends[block], 2, 1)
        whole = jnp.where(lane < 2, pltpu.roll(ends[block - 1], 2, 1), own)
        missing.append(products(whole) - products(jnp.where(lane < 2, 0.0, own)))
    return missing


def mix_kernel(in_ref, taps_ref, wave_ref, out_ref):
    top = lax.broadcasted_iota(jnp.int32, (8, N2), 0) < 4
    missing = edge_terms(in_ref, taps_ref)
    wave = wave_ref[lax.axis_index("seq")]
    for pair in range(2):
        sums = []
        for side in range(2):
            row = 4 + 2 * pair + side
            data, filt = [], []
            for block in range(SLICES):
                both = in_ref[block, 16 * pair : 16 * pair + 16, :].astype(f32)
                tile = both[8 * side : 8 * side + 8]
                if block:
                    lack = missing[block][row : row + 1]
                    tile = tile + jnp.where(top, lack[:, 0:1], 0.0) + lack[:, 1:2] * wave
                data.append(tile)
                both = in_ref[block, 32 + 16 * pair : 48 + 16 * pair, :].astype(f32)
                filt.append(both[8 * side : 8 * side + 8])
            swapped = [pltpu.roll(tile, 4, 0) for tile in data]
            real_parts, imag_parts = [], []
            for m in range(SLICES):
                tile = filt[m]
                if m:
                    turned = pltpu.roll(filt[m - 1], 4, 0)
                    tile = tile + jnp.where(top, -turned, turned)
                turned = pltpu.roll(tile, 4, 0)
                real_parts.append(jnp.where(top, tile, turned))
                imag_parts.append(jnp.where(top, -turned, tile))
            row = []
            for d in range(SLICES):
                total = None
                for e in range(d + 1):
                    term = data[e] * real_parts[d - e] + swapped[e] * imag_parts[d - e]
                    total = term if total is None else total + term
                row.append(total)
            sums.append(row)
        for d in range(SLICES):
            out_ref[d, 16 * pair : 16 * pair + 16, :] = jnp.concatenate([sums[0][d], sums[1][d]], axis=0).astype(bf16)


def inverse_kernel(in_ref, queries_ref, direct_ref, outer_ref, cos_ref, sin_ref, inner_ref, out_ref):
    turned = []
    for pair in range(2):
        both = in_ref[:, 16 * pair : 16 * pair + 16, :].astype(f32)
        for side in range(2):
            tile = both[:, 8 * side : 8 * side + 8, :].reshape(2 * N1, N2)
            tile = inner_stage(tile, inner_ref[...])
            turned.append(tile * cos_ref[...] - halves_swapped(tile) * sin_ref[...])
    high, low = split(jnp.concatenate(turned, axis=1))
    stacked = jnp.concatenate([high, low, high], axis=0)
    convolved = jnp.dot(outer_ref[...], stacked, preferred_element_type=f32)
    for c in range(4):
        gated = queries_ref[c] * (convolved[:, N2 * c : N2 * (c + 1)] + direct_ref[c])
        gated = gated.astype(bf16)
        for copy in range(out_ref.shape[0]):
            out_ref[copy, N1 * c : N1 * (c + 1), :] = gated


def wave_table():
    row = np.arange(2 * N1)
    k1 = 4 * (row // 8) + row % 4
    angle = 2 * math.pi * (k1[:, None] + 64 * np.arange(N2)[None, :] + 0.25) / BLOCK
    imag = (row // 4) % 2 == 1
    return np.where(imag[:, None], -np.sin(angle), np.cos(angle)).astype(np.float32).reshape(SLICES, 8, N2)


vmem = pl.BlockSpec(memory_space=pltpu.VMEM)
smem = pl.BlockSpec(memory_space=pltpu.SMEM)
anywhere = pl.BlockSpec(memory_space=pl.ANY)


def call(kernel, specs, shape, dtype, *operands, scratch=()):
    if isinstance(shape, list):
        out_shape, out_specs = [jax.ShapeDtypeStruct(s, dtype) for s in shape], [vmem] * len(shape)
    else:
        out_shape, out_specs = jax.ShapeDtypeStruct(shape, dtype), vmem
    return pl.pallas_call(
        kernel,
        out_shape=out_shape,
        in_specs=specs,
        out_specs=out_specs,
        scratch_shapes=scratch,
        compiler_params=pltpu.CompilerParams(vmem_limit_bytes=32 << 20),
        cost_estimate=pl.CostEstimate(flops=1 << 24, bytes_accessed=1 << 20, transcendentals=0),
    )(*operands)


def gated_copies(features, short_taps, long_filter, skip_gain, copies):
    forward_outer, inverse_outer, turn_cos, turn_sin, forward_inner, inverse_inner = map(jnp.asarray, tables())
    held = (features, short_taps, long_filter, forward_outer, turn_cos, turn_sin, forward_inner)
    rows = pltpu.VMEM((8 * N1, N2), f32)
    spectra = call(
        forward_kernel,
        [anywhere] * 7,
        (SLICES, 80, N2),
        bf16,
        *held,
        scratch=[pltpu.VMEM(x.shape, x.dtype) for x in held] + [rows, pltpu.SemaphoreType.DMA((7,))],
    )
    spectra = lax.all_to_all(spectra, "seq", 0, 0, tiled=True)
    queries, direct = call(
        gate_kernel,
        [anywhere] * 3 + [smem],
        [(4, N1, N2)] * 2,
        f32,
        features,
        short_taps,
        spectra,
        skip_gain,
        scratch=[
            pltpu.VMEM(features.shape, bf16),
            pltpu.VMEM(short_taps.shape, f32),
            pltpu.VMEM((16, N2), bf16),
            rows,
            pltpu.SemaphoreType.DMA((3,)),
        ],
    )
    mixed = call(
        mix_kernel, [vmem] * 3, (SLICES, 32, N2), bf16, spectra, short_taps, jnp.asarray(wave_table())
    )
    mixed = lax.all_to_all(mixed, "seq", 0, 0, tiled=True)
    return call(
        inverse_kernel,
        [vmem] * 7,
        (copies, 4 * N1, N2),
        bf16,
        mixed,
        queries,
        direct,
        inverse_outer,
        turn_cos,
        turn_sin,
        inverse_inner,
    )


def shards(features, short_taps, long_filter, skip_gain, out_weight):
    chan = lax.axis_size("chan")
    chips = chan // 2
    sent = gated_copies(features, short_taps, long_filter, skip_gain, chips)
    same_core = [[2 * chip + core for chip in range(chips)] for core in range(2)]
    own = lax.all_to_all(sent, "chan", 0, 0, tiled=True, axis_index_groups=same_core)
    other = lax.ppermute(own, "chan", [(d, d ^ 1) for d in range(chan)])
    core = lax.axis_index("chan") % 2
    weight = out_weight.reshape(chips, 2, 4, N2)
    own_weight = lax.dynamic_index_in_dim(weight, core, 1, False).reshape(4 * chips, N2)
    other_weight = lax.dynamic_index_in_dim(weight, 1 - core, 1, False).reshape(4 * chips, N2)
    rows = jnp.concatenate([own.reshape(4 * chips, BLOCK), other.reshape(4 * chips, BLOCK)], axis=0)
    weight = jnp.concatenate([own_weight, other_weight], axis=0)
    projected = lax.dot_general(rows, weight, (((0,), (0,)), ((), ())), preferred_element_type=f32)
    return projected.astype(bf16)


def solution(mesh):
    placed = (
        P(None, "chan", "seq"),
        P(None, "chan", None),
        P("chan", "seq"),
        P("chan"),
        P(None, "chan"),
    )
    return jax.shard_map(
        shards, mesh=mesh, in_specs=placed, out_specs=P("seq", "chan"), check_vma=False
    )
```

```python
import math

import jax
import jax.numpy as jnp
import ml_dtypes
import numpy as np
from jax import lax
from jax.experimental import pallas as pl
from jax.experimental.pallas import tpu as pltpu
from jax.sharding import PartitionSpec as P

N1, N2 = 64, 128
BLOCK = N1 * N2
SLICES = 16
f32, bf16 = jnp.float32, jnp.bfloat16


def split_table(table):
    high = table.astype(ml_dtypes.bfloat16)
    low = (table - high.astype(np.float64)).astype(ml_dtypes.bfloat16)
    return high, low


def tables():
    row = np.arange(2 * N1)
    k1 = 4 * (row // 8) + row % 4
    imag = (row // 4) % 2 == 1
    n1, n2 = np.arange(N1), np.arange(N2)
    phase = 2 * math.pi * np.outer(k1 + 0.25, n1) / N1
    outer = np.where(imag[:, None], -np.sin(phase), np.cos(phase))
    oh, ol = split_table(outer)
    forward_outer = np.concatenate([oh, oh, ol], axis=1)
    ih, il = split_table(outer.T / BLOCK)
    inverse_outer = np.concatenate([ih, ih, il], axis=1)
    angle = 2 * math.pi * np.outer(k1 + 0.25, n2) / BLOCK
    turn_cos = np.cos(angle).astype(np.float32)
    turn_sin = np.where(imag[:, None], -np.sin(angle), np.sin(angle)).astype(np.float32)
    phase = 2 * math.pi * np.outer(n2, n2) / N2

    def inner(sign):
        high, low = split_table(np.concatenate([np.cos(phase), sign * np.sin(phase)], axis=1))
        return np.concatenate([high, high, low], axis=0)

    return forward_outer, inverse_outer, turn_cos, turn_sin, inner(-1.0), inner(1.0)


def halves_swapped(tile):
    rows = tile.shape[0]
    return pltpu.roll(tile.reshape(rows // 8, 8, N2), 4, 1).reshape(rows, N2)


def split(value):
    high = value.astype(bf16)
    return high, (value - high.astype(f32)).astype(bf16)


def imag_sign(rows):
    return jnp.where(lax.broadcasted_iota(jnp.int32, (rows, N2), 0) % 8 < 4, -1.0, 1.0).astype(f32)


def inner_stage(rows, table):
    high, low = split(rows)
    both = jnp.dot(jnp.concatenate([high, low, high], axis=1), table, preferred_element_type=f32)
    return both[:, :N2] + imag_sign(rows.shape[0]) * halves_swapped(both[:, N2:])


def lane_index(shape):
    return lax.broadcasted_iota(jnp.int32, shape, 1)


def short_filter(stream, taps, edge=None):
    total = taps[:, 0:1] * stream
    for lag in (1, 2):
        turned = pltpu.roll(stream, lag, 1)
        head = turned[:, :N2]
        before = jnp.zeros_like(head) if edge is None else pltpu.roll(edge, lag, 1)
        head = jnp.where(lane_index(head.shape) < lag, before, head)
        total = total + taps[:, lag : lag + 1] * jnp.concatenate([head, turned[:, N2:]], axis=1)
    return total


def to_blocks(upper, lower, rows_ref):
    both = jnp.concatenate([upper, lower], axis=0)
    for n1 in range(N1):
        rows_ref[8 * n1 : 8 * n1 + 8, :] = both[:, N2 * n1 : N2 * (n1 + 1)]
    return [rows_ref[pl.ds(s, N1, stride=8), :] for s in range(8)]


def block_ends(streams, taps_ref):
    lane = lane_index((8, N2))
    first = jnp.concatenate([stream[:, :N2] for stream in streams[1:]], axis=0)
    last = jnp.concatenate([stream[:, BLOCK - N2 :] for stream in streams[1:]], axis=0)
    query = jnp.concatenate([streams[0][:, BLOCK - N2 :]] * 2, axis=0)
    taps = jnp.concatenate([taps_ref[1], taps_ref[2]], axis=0)
    own = taps[:, 0:1] * first + jnp.where(lane == 1, taps[:, 1:2] * pltpu.roll(first, 1, 1), 0.0)
    given = taps[:, 2:3] * last + jnp.where(lane == N2 - 2, taps[:, 1:2] * pltpu.roll(last, N2 - 1, 1), 0.0)
    exact = jnp.where(lane < 2, own, pltpu.roll(given, 4, 1))
    rest = exact - exact.astype(bf16).astype(f32)
    rest = jnp.where(lane < N1 + 4, pltpu.roll(rest, N1, 1), jnp.where(lane < N2 - 2, pltpu.roll(query, N2 - 2, 1), last))
    return jnp.where(lane < 4, exact, rest)


def forward_kernel(
    feat_hbm, taps_hbm, filt_hbm, outer_hbm, cos_hbm, sin_hbm, inner_hbm, out_ref,
    feat_ref, taps_ref, filt_ref, outer_ref, cos_ref, sin_ref, inner_ref, rows_ref, sems,
):
    sources = (feat_hbm, taps_hbm, filt_hbm, outer_hbm, cos_hbm, sin_hbm, inner_hbm)
    places = (feat_ref, taps_ref, filt_ref, outer_ref, cos_ref, sin_ref, inner_ref)
    copies = [pltpu.make_async_copy(s, d, sems.at[n]) for n, (s, d) in enumerate(zip(sources, places))]
    for copy in copies:
        copy.start()
    for copy in copies[:2]:
        copy.wait()
    streams = [feat_ref[i].astype(f32) for i in range(3)]
    ends = block_ends(streams, taps_ref).astype(bf16)
    for device in range(SLICES):
        out_ref[device, 64:72, :] = ends
    product = short_filter(streams[1], taps_ref[1]) * short_filter(streams[2], taps_ref[2])
    copies[2].wait()
    signals = to_blocks(product, filt_ref[...], rows_ref)
    high, low = split(jnp.concatenate(signals, axis=1))
    stacked = jnp.concatenate([high, low, high], axis=0)
    for copy in copies[3:]:
        copy.wait()
    first = jnp.dot(outer_ref[...], stacked, preferred_element_type=f32)
    for pair in range(4):
        done = []
        for s in (2 * pair, 2 * pair + 1):
            tile = first[:, N2 * s : N2 * (s + 1)]
            tile = tile * cos_ref[...] + halves_swapped(tile) * sin_ref[...]
            done.append(inner_stage(tile, inner_ref[...]).reshape(SLICES, 8, N2))
        out_ref[:, 16 * pair : 16 * pair + 16, :] = jnp.concatenate(done, axis=1).astype(bf16)


def gate_kernel(feat_hbm, taps_ref, spectra_ref, gain_ref, queries_ref, direct_ref, feat_ref, rows_ref, sem):
    copy = pltpu.make_async_copy(feat_hbm, feat_ref, sem)
    copy.start()
    device = lax.axis_index("seq")
    ends = spectra_ref[jnp.maximum(device - 1, 0), 64:72, :].astype(f32)
    ends = jnp.where(device > 0, ends, 0.0)
    edges = [pltpu.roll(ends, 2, 1)[:4], ends[:4], ends[4:]]
    copy.wait()
    mixed = [short_filter(feat_ref[i].astype(f32), taps_ref[i], edges[i]) for i in range(3)]
    rows = to_blocks(mixed[0], mixed[1] * mixed[2], rows_ref)
    for c in range(4):
        queries_ref[c] = rows[c]
        direct_ref[c] = gain_ref[c] * rows[4 + c]


def edge_terms(in_ref):
    missing, given = [None], None
    for block in range(SLICES):
        ends = in_ref[block, 64:72, :].astype(f32)
        own = ends + pltpu.roll(ends, N1, 1)
        if block:
            missing.append(own * pltpu.roll(given, 4, 0) + given * pltpu.roll(own + given, 4, 0))
        given = pltpu.roll(own, N2 - 2, 1)
    return missing


def wave_at(device):
    row = lax.broadcasted_iota(jnp.int32, (8, N2), 0)
    k = 4 * device + row % 4 + N1 * lane_index((8, N2))
    angle = (k.astype(f32) + 0.25) * (-2.0 * math.pi / BLOCK)
    return jnp.where(row < 4, jnp.cos(angle), jnp.sin(angle))


def mix_kernel(in_ref, out_ref):
    top = lax.broadcasted_iota(jnp.int32, (8, N2), 0) < 4
    missing = edge_terms(in_ref)
    wave = wave_at(lax.axis_index("seq"))
    for pair in range(2):
        sums = []
        for side in range(2):
            row = 2 * pair + side
            data, filt = [], []
            for block in range(SLICES):
                both = in_ref[block, 16 * pair : 16 * pair + 16, :].astype(f32)
                tile = both[8 * side : 8 * side + 8]
                if block:
                    lack = missing[block][row : row + 1]
                    tile = tile + jnp.where(top, lack[:, 0:1], 0.0) + lack[:, 1:2] * wave
                data.append(tile)
                both = in_ref[block, 32 + 16 * pair : 48 + 16 * pair, :].astype(f32)
                filt.append(both[8 * side : 8 * side + 8])
            swapped = [pltpu.roll(tile, 4, 0) for tile in data]
            real_parts, imag_parts = [], []
            for m in range(SLICES):
                tile = filt[m]
                if m:
                    turned = pltpu.roll(filt[m - 1], 4, 0)
                    tile = tile + jnp.where(top, -turned, turned)
                turned = pltpu.roll(tile, 4, 0)
                real_parts.append(jnp.where(top, tile, turned))
                imag_parts.append(jnp.where(top, -turned, tile))
            row = []
            for d in range(SLICES):
                total = None
                for e in range(d + 1):
                    term = data[e] * real_parts[d - e] + swapped[e] * imag_parts[d - e]
                    total = term if total is None else total + term
                row.append(total)
            sums.append(row)
        for d in range(SLICES):
            out_ref[d, 16 * pair : 16 * pair + 16, :] = jnp.concatenate([sums[0][d], sums[1][d]], axis=0).astype(bf16)


def inverse_kernel(in_ref, queries_ref, direct_ref, outer_ref, cos_ref, sin_ref, inner_ref, out_ref):
    turned = []
    for pair in range(2):
        both = in_ref[:, 16 * pair : 16 * pair + 16, :].astype(f32)
        for side in range(2):
            tile = both[:, 8 * side : 8 * side + 8, :].reshape(2 * N1, N2)
            tile = inner_stage(tile, inner_ref[...])
            turned.append(tile * cos_ref[...] - halves_swapped(tile) * sin_ref[...])
    high, low = split(jnp.concatenate(turned, axis=1))
    stacked = jnp.concatenate([high, low, high], axis=0)
    convolved = jnp.dot(outer_ref[...], stacked, preferred_element_type=f32)
    for c in range(4):
        gated = queries_ref[c] * (convolved[:, N2 * c : N2 * (c + 1)] + direct_ref[c])
        gated = gated.astype(bf16)
        for copy in range(out_ref.shape[0]):
            out_ref[copy, N1 * c : N1 * (c + 1), :] = gated


vmem = pl.BlockSpec(memory_space=pltpu.VMEM)
smem = pl.BlockSpec(memory_space=pltpu.SMEM)
hbm = pl.BlockSpec(memory_space=pltpu.HBM)


def call(kernel, specs, shape, dtype, *operands, scratch=(), grant=32 << 20):
    if isinstance(shape, list):
        out_shape, out_specs = [jax.ShapeDtypeStruct(s, d) for s, d in zip(shape, dtype)], [vmem] * len(shape)
    else:
        out_shape, out_specs = jax.ShapeDtypeStruct(shape, dtype), vmem
    return pl.pallas_call(
        kernel,
        out_shape=out_shape,
        in_specs=specs,
        out_specs=out_specs,
        scratch_shapes=scratch,
        compiler_params=pltpu.CompilerParams(vmem_limit_bytes=grant),
        cost_estimate=pl.CostEstimate(flops=1 << 24, bytes_accessed=1 << 20, transcendentals=0),
    )(*operands)


def gated_copies(features, short_taps, long_filter, skip_gain, copies):
    forward_outer, inverse_outer, turn_cos, turn_sin, forward_inner, inverse_inner = map(jnp.asarray, tables())
    held = (features, short_taps, long_filter, forward_outer, turn_cos, turn_sin, forward_inner)
    rows = pltpu.VMEM((8 * N1, N2), f32)
    spectra = call(
        forward_kernel,
        [hbm] * 7,
        (SLICES, 72, N2),
        bf16,
        features,
        short_taps,
        *held[2:],
        scratch=[pltpu.VMEM(x.shape, x.dtype) for x in held] + [rows, pltpu.SemaphoreType.DMA((7,))],
        grant=60 << 20,
    )
    spectra = lax.all_to_all(spectra, "seq", 0, 0, tiled=True)
    queries, direct = call(
        gate_kernel,
        [hbm, vmem, vmem, smem],
        [(4, N1, N2)] * 2,
        [f32] * 2,
        features,
        short_taps,
        spectra,
        skip_gain,
        scratch=[
            pltpu.VMEM(features.shape, bf16),
            rows,
            pltpu.SemaphoreType.DMA(()),
        ],
    )
    mixed = call(mix_kernel, [vmem], (SLICES, 32, N2), bf16, spectra)
    mixed = lax.all_to_all(mixed, "seq", 0, 0, tiled=True)
    return call(
        inverse_kernel,
        [vmem] * 7,
        (copies, 4 * N1, N2),
        bf16,
        mixed,
        queries,
        direct,
        inverse_outer,
        turn_cos,
        turn_sin,
        inverse_inner,
    )


def shards(features, short_taps, long_filter, skip_gain, out_weight):
    chan = lax.axis_size("chan")
    chips = chan // 2
    sent = gated_copies(features, short_taps, long_filter, skip_gain, chips)
    same_core = [[2 * chip + core for chip in range(chips)] for core in range(2)]
    own = lax.all_to_all(sent, "chan", 0, 0, tiled=True, axis_index_groups=same_core)
    other = lax.ppermute(own, "chan", [(d, d ^ 1) for d in range(chan)])
    core = lax.axis_index("chan") % 2
    weight = out_weight.reshape(chips, 2, 4, N2)
    own_weight = lax.dynamic_index_in_dim(weight, core, 1, False).reshape(4 * chips, N2)
    other_weight = lax.dynamic_index_in_dim(weight, 1 - core, 1, False).reshape(4 * chips, N2)
    rows = jnp.concatenate([own.reshape(4 * chips, BLOCK), other.reshape(4 * chips, BLOCK)], axis=0)
    weight = jnp.concatenate([own_weight, other_weight], axis=0)
    projected = lax.dot_general(rows, weight, (((0,), (0,)), ((), ())), preferred_element_type=f32)
    return projected.astype(bf16)


def solution(mesh):
    placed = (
        P(None, "chan", "seq"),
        P(None, "chan", None),
        P("chan", "seq"),
        P("chan"),
        P(None, "chan"),
    )
    return jax.shard_map(
        shards, mesh=mesh, in_specs=placed, out_specs=P("seq", "chan"), check_vma=False
    )
```

```python
import math

import jax
import jax.numpy as jnp
import ml_dtypes
import numpy as np
from jax import lax
from jax.experimental import pallas as pl
from jax.experimental.pallas import tpu as pltpu
from jax.sharding import PartitionSpec as P

N1, N2 = 64, 128
BLOCK = N1 * N2
SLICES = 16
OUT, BACK = 10, 8
FIRST_CHIP = 14
f32, bf16 = jnp.float32, jnp.bfloat16


def split_table(table):
    high = table.astype(ml_dtypes.bfloat16)
    low = (table - high.astype(np.float64)).astype(ml_dtypes.bfloat16)
    return high, low


def tables():
    row = np.arange(2 * N1)
    k1 = 4 * (row // 8) + row % 4
    imag = (row // 4) % 2 == 1
    n1, n2 = np.arange(N1), np.arange(N2)
    phase = 2 * math.pi * np.outer(k1 + 0.25, n1) / N1
    outer = np.where(imag[:, None], -np.sin(phase), np.cos(phase))
    oh, ol = split_table(outer)
    forward_outer = np.concatenate([oh, oh, ol], axis=1)
    ih, il = split_table(outer.T / BLOCK)
    inverse_outer = np.concatenate([ih, ih, il], axis=1)
    angle = 2 * math.pi * np.outer(k1 + 0.25, n2) / BLOCK
    turn_cos = np.cos(angle).astype(np.float32)
    turn_sin = np.where(imag[:, None], -np.sin(angle), np.sin(angle)).astype(np.float32)
    phase = 2 * math.pi * np.outer(n2, n2) / N2

    def inner(sign):
        high, low = split_table(np.concatenate([np.cos(phase), sign * np.sin(phase)], axis=1))
        return np.concatenate([high, high, low], axis=0)

    return forward_outer, inverse_outer, turn_cos, turn_sin, inner(-1.0), inner(1.0)


def halves_swapped(tile):
    rows = tile.shape[0]
    return pltpu.roll(tile.reshape(rows // 8, 8, N2), 4, 1).reshape(rows, N2)


def split(value):
    high = value.astype(bf16)
    return high, (value - high.astype(f32)).astype(bf16)


def imag_sign(rows):
    return jnp.where(lax.broadcasted_iota(jnp.int32, (rows, N2), 0) % 8 < 4, -1.0, 1.0).astype(f32)


def inner_stage(rows, table):
    high, low = split(rows)
    both = jnp.dot(jnp.concatenate([high, low, high], axis=1), table, preferred_element_type=f32)
    return both[:, :N2] + imag_sign(rows.shape[0]) * halves_swapped(both[:, N2:])


def lane_index(shape):
    return lax.broadcasted_iota(jnp.int32, shape, 1)


def short_filter(stream, taps, edge=None):
    total = taps[:, 0:1] * stream
    for lag in (1, 2):
        turned = pltpu.roll(stream, lag, 1)
        head = turned[:, :N2]
        before = jnp.zeros_like(head) if edge is None else pltpu.roll(edge, lag, 1)
        head = jnp.where(lane_index(head.shape) < lag, before, head)
        total = total + taps[:, lag : lag + 1] * jnp.concatenate([head, turned[:, N2:]], axis=1)
    return total


def to_blocks(upper, lower, rows_ref):
    both = jnp.concatenate([upper, lower], axis=0)
    for n1 in range(N1):
        rows_ref[8 * n1 : 8 * n1 + 8, :] = both[:, N2 * n1 : N2 * (n1 + 1)]
    return [rows_ref[pl.ds(s, N1, stride=8), :] for s in range(8)]


def block_ends(streams, taps_ref):
    lane = lane_index((8, N2))
    first = jnp.concatenate([stream[:, :N2] for stream in streams[1:]], axis=0)
    last = jnp.concatenate([stream[:, BLOCK - N2 :] for stream in streams[1:]], axis=0)
    query = jnp.concatenate([streams[0][:, BLOCK - N2 :]] * 2, axis=0)
    taps = jnp.concatenate([taps_ref[1], taps_ref[2]], axis=0)
    own = taps[:, 0:1] * first + jnp.where(lane == 1, taps[:, 1:2] * pltpu.roll(first, 1, 1), 0.0)
    given = taps[:, 2:3] * last + jnp.where(lane == N2 - 2, taps[:, 1:2] * pltpu.roll(last, N2 - 1, 1), 0.0)
    exact = jnp.where(lane < 2, own, pltpu.roll(given, 4, 1))
    rest = exact - exact.astype(bf16).astype(f32)
    rest = jnp.where(lane < N1 + 4, pltpu.roll(rest, N1, 1), jnp.where(lane < N2 - 2, pltpu.roll(query, N2 - 2, 1), last))
    return jnp.where(lane < 4, exact, rest)


def forward_kernel(
    feat_hbm, taps_hbm, filt_hbm, outer_hbm, cos_hbm, sin_hbm, inner_hbm, out_ref,
    feat_ref, taps_ref, filt_ref, outer_ref, cos_ref, sin_ref, inner_ref, rows_ref, sems,
):
    sources = (feat_hbm, taps_hbm, filt_hbm, outer_hbm, cos_hbm, sin_hbm, inner_hbm)
    places = (feat_ref, taps_ref, filt_ref, outer_ref, cos_ref, sin_ref, inner_ref)
    copies = [pltpu.make_async_copy(s, d, sems.at[n]) for n, (s, d) in enumerate(zip(sources, places))]
    for copy in copies:
        copy.start()
    for copy in copies[:2]:
        copy.wait()
    streams = [feat_ref[i].astype(f32) for i in range(3)]
    ends = block_ends(streams, taps_ref).astype(bf16)
    for device in range(SLICES):
        out_ref[device, 64:72, :] = ends
    product = short_filter(streams[1], taps_ref[1]) * short_filter(streams[2], taps_ref[2])
    copies[2].wait()
    signals = to_blocks(product, filt_ref[...], rows_ref)
    high, low = split(jnp.concatenate(signals, axis=1))
    stacked = jnp.concatenate([high, low, high], axis=0)
    for copy in copies[3:]:
        copy.wait()
    first = jnp.dot(outer_ref[...], stacked, preferred_element_type=f32)
    for pair in range(4):
        done = []
        for s in (2 * pair, 2 * pair + 1):
            tile = first[:, N2 * s : N2 * (s + 1)]
            tile = tile * cos_ref[...] + halves_swapped(tile) * sin_ref[...]
            done.append(inner_stage(tile, inner_ref[...]).reshape(SLICES, 8, N2))
        out_ref[:, 16 * pair : 16 * pair + 16, :] = jnp.concatenate(done, axis=1).astype(bf16)


def gate_kernel(feat_hbm, taps_ref, spectra_ref, gain_ref, queries_ref, direct_ref, feat_ref, rows_ref, sem):
    copy = pltpu.make_async_copy(feat_hbm, feat_ref, sem)
    copy.start()
    device = lax.axis_index("seq")
    ends = spectra_ref[(device + SLICES - 1 - OUT) % SLICES, 64:72, :].astype(f32)
    ends = jnp.where(device > 0, ends, 0.0)
    edges = [pltpu.roll(ends, 2, 1)[:4], ends[:4], ends[4:]]
    copy.wait()
    mixed = [short_filter(feat_ref[i].astype(f32), taps_ref[i], edges[i]) for i in range(3)]
    rows = to_blocks(mixed[0], mixed[1] * mixed[2], rows_ref)
    for c in range(4):
        queries_ref[c] = rows[c]
        direct_ref[c] = gain_ref[c] * rows[4 + c]


def slot(block, first):
    return (block - first) % SLICES


def over_seq(value, first):
    group = [(j + first) % SLICES for j in range(SLICES)]
    return lax.all_to_all(value, "seq", 0, 0, tiled=True, axis_index_groups=[group])


def edge_terms(in_ref):
    missing, given = [None], None
    for block in range(SLICES):
        ends = in_ref[slot(block, OUT), 64:72, :].astype(f32)
        own = ends + pltpu.roll(ends, N1, 1)
        if block:
            missing.append(own * pltpu.roll(given, 4, 0) + given * pltpu.roll(own + given, 4, 0))
        given = pltpu.roll(own, N2 - 2, 1)
    return missing


def wave_at(device):
    row = lax.broadcasted_iota(jnp.int32, (8, N2), 0)
    k = 4 * device + row % 4 + N1 * lane_index((8, N2))
    angle = (k.astype(f32) + 0.25) * (-2.0 * math.pi / BLOCK)
    return jnp.where(row < 4, jnp.cos(angle), jnp.sin(angle))


def mix_kernel(in_ref, out_ref):
    top = lax.broadcasted_iota(jnp.int32, (8, N2), 0) < 4
    missing = edge_terms(in_ref)
    wave = wave_at((lax.axis_index("seq") + SLICES - OUT) % SLICES)
    for pair in range(2):
        sums = []
        for side in range(2):
            row = 2 * pair + side
            data, filt = [], []
            for block in range(SLICES):
                both = in_ref[slot(block, OUT), 16 * pair : 16 * pair + 16, :].astype(f32)
                tile = both[8 * side : 8 * side + 8]
                if block:
                    lack = missing[block][row : row + 1]
                    tile = tile + jnp.where(top, lack[:, 0:1], 0.0) + lack[:, 1:2] * wave
                data.append(tile)
                both = in_ref[slot(block, OUT), 32 + 16 * pair : 48 + 16 * pair, :].astype(f32)
                filt.append(both[8 * side : 8 * side + 8])
            swapped = [pltpu.roll(tile, 4, 0) for tile in data]
            real_parts, imag_parts = [], []
            for m in range(SLICES):
                tile = filt[m]
                if m:
                    turned = pltpu.roll(filt[m - 1], 4, 0)
                    tile = tile + jnp.where(top, -turned, turned)
                turned = pltpu.roll(tile, 4, 0)
                real_parts.append(jnp.where(top, tile, turned))
                imag_parts.append(jnp.where(top, -turned, tile))
            row = []
            for d in range(SLICES):
                total = None
                for e in range(d + 1):
                    term = data[e] * real_parts[d - e] + swapped[e] * imag_parts[d - e]
                    total = term if total is None else total + term
                row.append(total)
            sums.append(row)
        for d in range(SLICES):
            out_ref[slot(d, BACK), 16 * pair : 16 * pair + 16, :] = jnp.concatenate([sums[0][d], sums[1][d]], axis=0).astype(bf16)


def inverse_kernel(in_ref, queries_ref, direct_ref, outer_ref, cos_ref, sin_ref, inner_ref, out_ref):
    turned = []
    for pair in range(2):
        both = [in_ref[slot(p + OUT, BACK), 16 * pair : 16 * pair + 16, :].astype(f32) for p in range(SLICES)]
        for side in range(2):
            tile = jnp.concatenate([part[8 * side : 8 * side + 8] for part in both], axis=0)
            tile = inner_stage(tile, inner_ref[...])
            turned.append(tile * cos_ref[...] - halves_swapped(tile) * sin_ref[...])
    high, low = split(jnp.concatenate(turned, axis=1))
    stacked = jnp.concatenate([high, low, high], axis=0)
    convolved = jnp.dot(outer_ref[...], stacked, preferred_element_type=f32)
    for c in range(4):
        gated = queries_ref[c] * (convolved[:, N2 * c : N2 * (c + 1)] + direct_ref[c])
        gated = gated.astype(bf16)
        for copy in range(out_ref.shape[0]):
            out_ref[copy, N1 * c : N1 * (c + 1), :] = gated


vmem = pl.BlockSpec(memory_space=pltpu.VMEM)
smem = pl.BlockSpec(memory_space=pltpu.SMEM)
hbm = pl.BlockSpec(memory_space=pltpu.HBM)


def call(kernel, specs, shape, dtype, *operands, scratch=(), grant=32 << 20):
    if isinstance(shape, list):
        out_shape, out_specs = [jax.ShapeDtypeStruct(s, d) for s, d in zip(shape, dtype)], [vmem] * len(shape)
    else:
        out_shape, out_specs = jax.ShapeDtypeStruct(shape, dtype), vmem
    return pl.pallas_call(
        kernel,
        out_shape=out_shape,
        in_specs=specs,
        out_specs=out_specs,
        scratch_shapes=scratch,
        compiler_params=pltpu.CompilerParams(vmem_limit_bytes=grant),
        cost_estimate=pl.CostEstimate(flops=1 << 24, bytes_accessed=1 << 20, transcendentals=0),
    )(*operands)


def gated_copies(features, short_taps, long_filter, skip_gain, copies):
    forward_outer, inverse_outer, turn_cos, turn_sin, forward_inner, inverse_inner = map(jnp.asarray, tables())
    held = (features, short_taps, long_filter, forward_outer, turn_cos, turn_sin, forward_inner)
    rows = pltpu.VMEM((8 * N1, N2), f32)
    spectra = call(
        forward_kernel,
        [hbm] * 7,
        (SLICES, 72, N2),
        bf16,
        features,
        short_taps,
        *held[2:],
        scratch=[pltpu.VMEM(x.shape, x.dtype) for x in held] + [rows, pltpu.SemaphoreType.DMA((7,))],
        grant=60 << 20,
    )
    spectra = over_seq(spectra, OUT)
    queries, direct = call(
        gate_kernel,
        [hbm, vmem, vmem, smem],
        [(4, N1, N2)] * 2,
        [f32] * 2,
        features,
        short_taps,
        spectra,
        skip_gain,
        scratch=[
            pltpu.VMEM(features.shape, bf16),
            rows,
            pltpu.SemaphoreType.DMA(()),
        ],
    )
    mixed = call(mix_kernel, [vmem], (SLICES, 32, N2), bf16, spectra)
    mixed = over_seq(mixed, BACK)
    return call(
        inverse_kernel,
        [vmem] * 7,
        (copies, 4 * N1, N2),
        bf16,
        mixed,
        queries,
        direct,
        inverse_outer,
        turn_cos,
        turn_sin,
        inverse_inner,
    )


def gather_groups(chips):
    order = [(chip + FIRST_CHIP) % chips for chip in range(chips)]
    return [[2 * chip + core for chip in order] for core in range(2)]


def shards(features, short_taps, long_filter, skip_gain, out_weight):
    chan = lax.axis_size("chan")
    chips = chan // 2
    groups = gather_groups(chips)
    sent = gated_copies(features, short_taps, long_filter, skip_gain, chips)
    own = lax.all_to_all(sent, "chan", 0, 0, tiled=True, axis_index_groups=groups)
    other = lax.ppermute(own, "chan", [(d, d ^ 1) for d in range(chan)])
    blocks = out_weight.reshape(chan, 4, N2)
    sides = [jnp.concatenate([blocks[d] for d in groups[g] + groups[1 - g]], axis=0) for g in range(2)]
    weight = jnp.where(lax.axis_index("chan") % 2 == 0, sides[0], sides[1])
    rows = jnp.concatenate([own.reshape(4 * chips, BLOCK), other.reshape(4 * chips, BLOCK)], axis=0)
    projected = lax.dot_general(rows, weight, (((0,), (0,)), ((), ())), preferred_element_type=f32)
    return projected.astype(bf16)


def solution(mesh):
    placed = (
        P(None, "chan", "seq"),
        P(None, "chan", None),
        P("chan", "seq"),
        P("chan"),
        P(None, "chan"),
    )
    return jax.shard_map(
        shards, mesh=mesh, in_specs=placed, out_specs=P("seq", "chan"), check_vma=False
    )
```

```python
import math

import jax
import jax.numpy as jnp
import ml_dtypes
import numpy as np
from jax import lax
from jax.experimental import pallas as pl
from jax.experimental.pallas import tpu as pltpu
from jax.sharding import PartitionSpec as P

N1, N2 = 64, 128
BLOCK = N1 * N2
SLICES = 16
OUT, BACK = 12, 8
FIRST_CHIP = 14
f32, bf16 = jnp.float32, jnp.bfloat16


def split_table(table):
    high = table.astype(ml_dtypes.bfloat16)
    low = (table - high.astype(np.float64)).astype(ml_dtypes.bfloat16)
    return high, low


def tables():
    row = np.arange(2 * N1)
    k1 = 4 * (row // 8) + row % 4
    imag = (row // 4) % 2 == 1
    n1, n2 = np.arange(N1), np.arange(N2)
    phase = 2 * math.pi * np.outer(k1 + 0.25, n1) / N1
    outer = np.where(imag[:, None], -np.sin(phase), np.cos(phase))
    oh, ol = split_table(outer)
    forward_outer = np.concatenate([oh, oh, ol], axis=1)
    ih, il = split_table(outer.T / BLOCK)
    inverse_outer = np.concatenate([ih, ih, il], axis=1)
    angle = 2 * math.pi * np.outer(k1 + 0.25, n2) / BLOCK
    turn_cos = np.cos(angle).astype(np.float32)
    turn_sin = np.where(imag[:, None], -np.sin(angle), np.sin(angle)).astype(np.float32)
    phase = 2 * math.pi * np.outer(n2, n2) / N2

    def inner(sign):
        high, low = split_table(np.concatenate([np.cos(phase), sign * np.sin(phase)], axis=1))
        return np.concatenate([high, high, low], axis=0)

    return forward_outer, inverse_outer, turn_cos, turn_sin, inner(-1.0), inner(1.0)


def halves_swapped(tile):
    rows = tile.shape[0]
    return pltpu.roll(tile.reshape(rows // 8, 8, N2), 4, 1).reshape(rows, N2)


def split(value):
    high = value.astype(bf16)
    return high, (value - high.astype(f32)).astype(bf16)


def imag_sign(rows):
    return jnp.where(lax.broadcasted_iota(jnp.int32, (rows, N2), 0) % 8 < 4, -1.0, 1.0).astype(f32)


def inner_stage(rows, table):
    high, low = split(rows)
    both = jnp.dot(jnp.concatenate([high, low, high], axis=1), table, preferred_element_type=f32)
    return both[:, :N2] + imag_sign(rows.shape[0]) * halves_swapped(both[:, N2:])


def lane_index(shape):
    return lax.broadcasted_iota(jnp.int32, shape, 1)


def short_filter(stream, taps, edge=None):
    total = taps[:, 0:1] * stream
    for lag in (1, 2):
        turned = pltpu.roll(stream, lag, 1)
        head = turned[:, :N2]
        before = jnp.zeros_like(head) if edge is None else pltpu.roll(edge, lag, 1)
        head = jnp.where(lane_index(head.shape) < lag, before, head)
        total = total + taps[:, lag : lag + 1] * jnp.concatenate([head, turned[:, N2:]], axis=1)
    return total


def to_blocks(upper, lower, rows_ref):
    both = jnp.concatenate([upper, lower], axis=0)
    for n1 in range(N1):
        rows_ref[8 * n1 : 8 * n1 + 8, :] = both[:, N2 * n1 : N2 * (n1 + 1)]
    return [rows_ref[pl.ds(s, N1, stride=8), :] for s in range(8)]


def block_ends(query, streams, taps_ref):
    lane = lane_index((8, N2))
    first = jnp.concatenate([stream[:, :N2] for stream in streams], axis=0)
    last = jnp.concatenate([stream[:, BLOCK - N2 :] for stream in streams], axis=0)
    query = jnp.concatenate([query] * 2, axis=0)
    taps = jnp.concatenate([taps_ref[1], taps_ref[2]], axis=0)
    own = taps[:, 0:1] * first + jnp.where(lane == 1, taps[:, 1:2] * pltpu.roll(first, 1, 1), 0.0)
    given = taps[:, 2:3] * last + jnp.where(lane == N2 - 2, taps[:, 1:2] * pltpu.roll(last, N2 - 1, 1), 0.0)
    exact = jnp.where(lane < 2, own, pltpu.roll(given, 4, 1))
    rest = exact - exact.astype(bf16).astype(f32)
    rest = jnp.where(lane < N1 + 4, pltpu.roll(rest, N1, 1), jnp.where(lane < N2 - 2, pltpu.roll(query, N2 - 2, 1), last))
    return jnp.where(lane < 4, exact, rest)


def forward_kernel(
    feat_hbm, taps_hbm, filt_hbm, outer_hbm, cos_hbm, sin_hbm, inner_hbm, out_ref,
    feat_ref, taps_ref, filt_ref, outer_ref, cos_ref, sin_ref, inner_ref, last_ref, rows_ref, sems,
):
    last = pl.ds(BLOCK - N2, N2)
    sources = (feat_hbm.at[1:3], filt_hbm, taps_hbm, feat_hbm.at[0, :, last], outer_hbm, inner_hbm, cos_hbm, sin_hbm)
    places = (feat_ref, filt_ref, taps_ref, last_ref, outer_ref, inner_ref, cos_ref, sin_ref)
    copies = [pltpu.make_async_copy(s, d, sems.at[n]) for n, (s, d) in enumerate(zip(sources, places))]
    for copy in copies:
        copy.start()
    for copy in copies[:4]:
        copy.wait()
    streams = [feat_ref[i].astype(f32) for i in range(2)]
    ends = block_ends(last_ref[...].astype(f32), streams, taps_ref).astype(bf16)
    for device in range(SLICES):
        out_ref[device, 64:72, :] = ends
    product = short_filter(streams[0], taps_ref[1]) * short_filter(streams[1], taps_ref[2])
    signals = to_blocks(product, filt_ref[...], rows_ref)
    high, low = split(jnp.concatenate(signals, axis=1))
    stacked = jnp.concatenate([high, low, high], axis=0)
    for copy in copies[4:]:
        copy.wait()
    first = jnp.dot(outer_ref[...], stacked, preferred_element_type=f32)
    for pair in range(4):
        done = []
        for s in (2 * pair, 2 * pair + 1):
            tile = first[:, N2 * s : N2 * (s + 1)]
            tile = tile * cos_ref[...] + halves_swapped(tile) * sin_ref[...]
            done.append(inner_stage(tile, inner_ref[...]).reshape(SLICES, 8, N2))
        out_ref[:, 16 * pair : 16 * pair + 16, :] = jnp.concatenate(done, axis=1).astype(bf16)


def gate_kernel(feat_hbm, taps_ref, spectra_ref, gain_ref, queries_ref, direct_ref, feat_ref, rows_ref, sem):
    copy = pltpu.make_async_copy(feat_hbm, feat_ref, sem)
    copy.start()
    device = lax.axis_index("seq")
    ends = spectra_ref[(device + SLICES - 1 - OUT) % SLICES, 64:72, :].astype(f32)
    ends = jnp.where(device > 0, ends, 0.0)
    edges = [pltpu.roll(ends, 2, 1)[:4], ends[:4], ends[4:]]
    copy.wait()
    mixed = [short_filter(feat_ref[i].astype(f32), taps_ref[i], edges[i]) for i in range(3)]
    rows = to_blocks(mixed[0], mixed[1] * mixed[2], rows_ref)
    for c in range(4):
        queries_ref[c] = rows[c]
        direct_ref[c] = gain_ref[c] * rows[4 + c]


def slot(block, first):
    return (block - first) % SLICES


def over_seq(value, first):
    group = [(j + first) % SLICES for j in range(SLICES)]
    return lax.all_to_all(value, "seq", 0, 0, tiled=True, axis_index_groups=[group])


def edge_terms(in_ref):
    missing, given = [None], None
    for block in range(SLICES):
        ends = in_ref[slot(block, OUT), 64:72, :].astype(f32)
        own = ends + pltpu.roll(ends, N1, 1)
        if block:
            missing.append(own * pltpu.roll(given, 4, 0) + given * pltpu.roll(own + given, 4, 0))
        given = pltpu.roll(own, N2 - 2, 1)
    return missing


def wave_at(device):
    row = lax.broadcasted_iota(jnp.int32, (8, N2), 0)
    k = 4 * device + row % 4 + N1 * lane_index((8, N2))
    angle = (k.astype(f32) + 0.25) * (-2.0 * math.pi / BLOCK)
    return jnp.where(row < 4, jnp.cos(angle), jnp.sin(angle))


def mix_kernel(in_ref, out_ref):
    top = lax.broadcasted_iota(jnp.int32, (8, N2), 0) < 4
    missing = edge_terms(in_ref)
    wave = wave_at((lax.axis_index("seq") + SLICES - OUT) % SLICES)
    for pair in range(2):
        sums = []
        for side in range(2):
            row = 2 * pair + side
            data, filt = [], []
            for block in range(SLICES):
                both = in_ref[slot(block, OUT), 16 * pair : 16 * pair + 16, :].astype(f32)
                tile = both[8 * side : 8 * side + 8]
                if block:
                    lack = missing[block][row : row + 1]
                    tile = tile + jnp.where(top, lack[:, 0:1], 0.0) + lack[:, 1:2] * wave
                data.append(tile)
                both = in_ref[slot(block, OUT), 32 + 16 * pair : 48 + 16 * pair, :].astype(f32)
                filt.append(both[8 * side : 8 * side + 8])
            swapped = [pltpu.roll(tile, 4, 0) for tile in data]
            real_parts, imag_parts = [], []
            for m in range(SLICES):
                tile = filt[m]
                if m:
                    turned = pltpu.roll(filt[m - 1], 4, 0)
                    tile = tile + jnp.where(top, -turned, turned)
                turned = pltpu.roll(tile, 4, 0)
                real_parts.append(jnp.where(top, tile, turned))
                imag_parts.append(jnp.where(top, -turned, tile))
            row = []
            for d in range(SLICES):
                total = None
                for e in range(d + 1):
                    term = data[e] * real_parts[d - e] + swapped[e] * imag_parts[d - e]
                    total = term if total is None else total + term
                row.append(total)
            sums.append(row)
        for d in range(SLICES):
            out_ref[slot(d, BACK), 16 * pair : 16 * pair + 16, :] = jnp.concatenate([sums[0][d], sums[1][d]], axis=0).astype(bf16)


def inverse_kernel(in_ref, queries_ref, direct_ref, outer_ref, cos_ref, sin_ref, inner_ref, out_ref):
    turned = []
    for pair in range(2):
        both = [in_ref[slot(p + OUT, BACK), 16 * pair : 16 * pair + 16, :].astype(f32) for p in range(SLICES)]
        for side in range(2):
            tile = jnp.concatenate([part[8 * side : 8 * side + 8] for part in both], axis=0)
            tile = inner_stage(tile, inner_ref[...])
            turned.append(tile * cos_ref[...] - halves_swapped(tile) * sin_ref[...])
    high, low = split(jnp.concatenate(turned, axis=1))
    stacked = jnp.concatenate([high, low, high], axis=0)
    convolved = jnp.dot(outer_ref[...], stacked, preferred_element_type=f32)
    for c in range(4):
        gated = queries_ref[c] * (convolved[:, N2 * c : N2 * (c + 1)] + direct_ref[c])
        gated = gated.astype(bf16)
        for copy in range(out_ref.shape[0]):
            out_ref[copy, N1 * c : N1 * (c + 1), :] = gated


vmem = pl.BlockSpec(memory_space=pltpu.VMEM)
smem = pl.BlockSpec(memory_space=pltpu.SMEM)
hbm = pl.BlockSpec(memory_space=pltpu.HBM)


def call(kernel, specs, shape, dtype, *operands, scratch=(), grant=32 << 20):
    if isinstance(shape, list):
        out_shape, out_specs = [jax.ShapeDtypeStruct(s, d) for s, d in zip(shape, dtype)], [vmem] * len(shape)
    else:
        out_shape, out_specs = jax.ShapeDtypeStruct(shape, dtype), vmem
    return pl.pallas_call(
        kernel,
        out_shape=out_shape,
        in_specs=specs,
        out_specs=out_specs,
        scratch_shapes=scratch,
        compiler_params=pltpu.CompilerParams(vmem_limit_bytes=grant),
        cost_estimate=pl.CostEstimate(flops=1 << 24, bytes_accessed=1 << 20, transcendentals=0),
    )(*operands)


def gated_copies(features, short_taps, long_filter, skip_gain, copies):
    forward_outer, inverse_outer, turn_cos, turn_sin, forward_inner, inverse_inner = map(jnp.asarray, tables())
    held = (features, short_taps, long_filter, forward_outer, turn_cos, turn_sin, forward_inner)
    held = [pltpu.with_memory_space_constraint(x, pltpu.HBM) for x in held]
    rows = pltpu.VMEM((8 * N1, N2), f32)
    spectra = call(
        forward_kernel,
        [hbm] * 7,
        (SLICES, 72, N2),
        bf16,
        *held,
        scratch=[pltpu.VMEM((2, 4, BLOCK), bf16)]
        + [pltpu.VMEM(x.shape, x.dtype) for x in held[1:]]
        + [pltpu.VMEM((4, N2), bf16), rows, pltpu.SemaphoreType.DMA((8,))],
    )
    spectra = over_seq(spectra, OUT)
    queries, direct = call(
        gate_kernel,
        [hbm, vmem, vmem, smem],
        [(4, N1, N2)] * 2,
        [f32] * 2,
        features,
        short_taps,
        spectra,
        skip_gain,
        scratch=[
            pltpu.VMEM(features.shape, bf16),
            rows,
            pltpu.SemaphoreType.DMA(()),
        ],
    )
    mixed = call(mix_kernel, [vmem], (SLICES, 32, N2), bf16, spectra)
    mixed = over_seq(mixed, BACK)
    return call(
        inverse_kernel,
        [vmem] * 7,
        (copies, 4 * N1, N2),
        bf16,
        mixed,
        queries,
        direct,
        inverse_outer,
        turn_cos,
        turn_sin,
        inverse_inner,
    )


def gather_groups(chips):
    order = [(chip + FIRST_CHIP) % chips for chip in range(chips)]
    return [[2 * chip + core for chip in order] for core in range(2)]


def shards(features, short_taps, long_filter, skip_gain, out_weight):
    chan = lax.axis_size("chan")
    chips = chan // 2
    groups = gather_groups(chips)
    sent = gated_copies(features, short_taps, long_filter, skip_gain, chips)
    own = lax.all_to_all(sent, "chan", 0, 0, tiled=True, axis_index_groups=groups)
    other = lax.ppermute(own, "chan", [(d, d ^ 1) for d in range(chan)])
    blocks = out_weight.reshape(chan, 4, N2)
    sides = [jnp.concatenate([blocks[d] for d in groups[g] + groups[1 - g]], axis=0) for g in range(2)]
    weight = jnp.where(lax.axis_index("chan") % 2 == 0, sides[0], sides[1])
    rows = jnp.concatenate([own.reshape(4 * chips, BLOCK), other.reshape(4 * chips, BLOCK)], axis=0)
    projected = lax.dot_general(rows, weight, (((0,), (0,)), ((), ())), preferred_element_type=f32)
    return projected.astype(bf16)


def solution(mesh):
    placed = (
        P(None, "chan", "seq"),
        P(None, "chan", None),
        P("chan", "seq"),
        P("chan"),
        P(None, "chan"),
    )
    return jax.shard_map(
        shards, mesh=mesh, in_specs=placed, out_specs=P("seq", "chan"), check_vma=False
    )
```

```python
import math

import jax
import jax.numpy as jnp
import ml_dtypes
import numpy as np
from jax import lax
from jax.experimental import pallas as pl
from jax.experimental.pallas import tpu as pltpu
from jax.sharding import PartitionSpec as P

N1, N2 = 64, 128
BLOCK = N1 * N2
SLICES = 16
OUT = [(j + 12) % SLICES for j in range(SLICES)]
BACK = [8, 0, 1, 15, 2, 14, 3, 13, 4, 12, 5, 11, 6, 10, 7, 9]
CHIPS = [(j + 14) % 16 for j in range(16)]
f32, bf16 = jnp.float32, jnp.bfloat16


def split_table(table):
    high = table.astype(ml_dtypes.bfloat16)
    low = (table - high.astype(np.float64)).astype(ml_dtypes.bfloat16)
    return high, low


def tables():
    row = np.arange(2 * N1)
    k1 = 4 * (row // 8) + row % 4
    imag = (row // 4) % 2 == 1
    n1, n2 = np.arange(N1), np.arange(N2)
    phase = 2 * math.pi * np.outer(k1 + 0.25, n1) / N1
    outer = np.where(imag[:, None], -np.sin(phase), np.cos(phase))
    oh, ol = split_table(outer)
    forward_outer = np.concatenate([oh, oh, ol], axis=1)
    ih, il = split_table(outer.T / BLOCK)
    inverse_outer = np.concatenate([ih, ih, il], axis=1)
    angle = 2 * math.pi * np.outer(k1 + 0.25, n2) / BLOCK
    turn_cos = np.cos(angle).astype(np.float32)
    turn_sin = np.where(imag[:, None], -np.sin(angle), np.sin(angle)).astype(np.float32)
    phase = 2 * math.pi * np.outer(n2, n2) / N2

    def inner(sign):
        high, low = split_table(np.concatenate([np.cos(phase), sign * np.sin(phase)], axis=1))
        return np.concatenate([high, high, low], axis=0)

    return forward_outer, inverse_outer, turn_cos, turn_sin, inner(-1.0), inner(1.0)


def halves_swapped(tile):
    rows = tile.shape[0]
    return pltpu.roll(tile.reshape(rows // 8, 8, N2), 4, 1).reshape(rows, N2)


def split(value):
    high = value.astype(bf16)
    return high, (value - high.astype(f32)).astype(bf16)


def imag_sign(rows):
    return jnp.where(lax.broadcasted_iota(jnp.int32, (rows, N2), 0) % 8 < 4, -1.0, 1.0).astype(f32)


def inner_stage(rows, table):
    high, low = split(rows)
    both = jnp.dot(jnp.concatenate([high, low, high], axis=1), table, preferred_element_type=f32)
    return both[:, :N2] + imag_sign(rows.shape[0]) * halves_swapped(both[:, N2:])


def lane_index(shape):
    return lax.broadcasted_iota(jnp.int32, shape, 1)


def short_filter(stream, taps, edge=None):
    total = taps[:, 0:1] * stream
    for lag in (1, 2):
        turned = pltpu.roll(stream, lag, 1)
        head = turned[:, :N2]
        before = jnp.zeros_like(head) if edge is None else pltpu.roll(edge, lag, 1)
        head = jnp.where(lane_index(head.shape) < lag, before, head)
        total = total + taps[:, lag : lag + 1] * jnp.concatenate([head, turned[:, N2:]], axis=1)
    return total


def to_blocks(upper, lower, rows_ref):
    both = jnp.concatenate([upper, lower], axis=0)
    for n1 in range(N1):
        rows_ref[8 * n1 : 8 * n1 + 8, :] = both[:, N2 * n1 : N2 * (n1 + 1)]
    return [rows_ref[pl.ds(s, N1, stride=8), :] for s in range(8)]


def block_ends(query, streams, taps_ref):
    lane = lane_index((8, N2))
    first = jnp.concatenate([stream[:, :N2] for stream in streams], axis=0)
    last = jnp.concatenate([stream[:, BLOCK - N2 :] for stream in streams], axis=0)
    query = jnp.concatenate([query] * 2, axis=0)
    taps = jnp.concatenate([taps_ref[1], taps_ref[2]], axis=0)
    own = taps[:, 0:1] * first + jnp.where(lane == 1, taps[:, 1:2] * pltpu.roll(first, 1, 1), 0.0)
    given = taps[:, 2:3] * last + jnp.where(lane == N2 - 2, taps[:, 1:2] * pltpu.roll(last, N2 - 1, 1), 0.0)
    exact = jnp.where(lane < 2, own, pltpu.roll(given, 4, 1))
    rest = exact - exact.astype(bf16).astype(f32)
    rest = jnp.where(lane < N1 + 4, pltpu.roll(rest, N1, 1), jnp.where(lane < N2 - 2, pltpu.roll(query, N2 - 2, 1), last))
    return jnp.where(lane < 4, exact, rest)


def forward_kernel(
    feat_hbm, taps_hbm, filt_hbm, outer_hbm, cos_hbm, sin_hbm, inner_hbm, out_ref,
    feat_ref, taps_ref, filt_ref, outer_ref, cos_ref, sin_ref, inner_ref, last_ref, rows_ref, sems,
):
    last = pl.ds(BLOCK - N2, N2)
    sources = (feat_hbm.at[1:3], filt_hbm, taps_hbm, feat_hbm.at[0, :, last], outer_hbm, inner_hbm, cos_hbm, sin_hbm)
    places = (feat_ref, filt_ref, taps_ref, last_ref, outer_ref, inner_ref, cos_ref, sin_ref)
    copies = [pltpu.make_async_copy(s, d, sems.at[n]) for n, (s, d) in enumerate(zip(sources, places))]
    for copy in copies:
        copy.start()
    for copy in copies[:4]:
        copy.wait()
    streams = [feat_ref[i].astype(f32) for i in range(2)]
    ends = block_ends(last_ref[...].astype(f32), streams, taps_ref).astype(bf16)
    for device in range(SLICES):
        out_ref[device, 64:72, :] = ends
    product = short_filter(streams[0], taps_ref[1]) * short_filter(streams[1], taps_ref[2])
    signals = to_blocks(product, filt_ref[...], rows_ref)
    high, low = split(jnp.concatenate(signals, axis=1))
    stacked = jnp.concatenate([high, low, high], axis=0)
    for copy in copies[4:]:
        copy.wait()
    first = jnp.dot(outer_ref[...], stacked, preferred_element_type=f32)
    for pair in range(4):
        done = []
        for s in (2 * pair, 2 * pair + 1):
            tile = first[:, N2 * s : N2 * (s + 1)]
            tile = tile * cos_ref[...] + halves_swapped(tile) * sin_ref[...]
            done.append(inner_stage(tile, inner_ref[...]).reshape(SLICES, 8, N2))
        out_ref[:, 16 * pair : 16 * pair + 16, :] = jnp.concatenate(done, axis=1).astype(bf16)


def gate_kernel(feat_hbm, taps_ref, spectra_ref, gain_ref, queries_ref, direct_ref, feat_ref, rows_ref, sem):
    copy = pltpu.make_async_copy(feat_hbm, feat_ref, sem)
    copy.start()
    device = lax.axis_index("seq")
    ends = spectra_ref[slot(jnp.maximum(device - 1, 0), OUT), 64:72, :].astype(f32)
    ends = jnp.where(device > 0, ends, 0.0)
    edges = [pltpu.roll(ends, 2, 1)[:4], ends[:4], ends[4:]]
    copy.wait()
    mixed = [short_filter(feat_ref[i].astype(f32), taps_ref[i], edges[i]) for i in range(3)]
    rows = to_blocks(mixed[0], mixed[1] * mixed[2], rows_ref)
    for c in range(4):
        queries_ref[c] = rows[c]
        direct_ref[c] = gain_ref[c] * rows[4 + c]


def slot(device, order):
    if isinstance(device, int):
        return order.index(device)
    return sum(jnp.where(device == z, j, 0) for j, z in enumerate(order))


def over_seq(value, order):
    return lax.all_to_all(value, "seq", 0, 0, tiled=True, axis_index_groups=[order])


def edge_terms(in_ref):
    missing, given = [None], None
    for block in range(SLICES):
        ends = in_ref[slot(block, OUT), 64:72, :].astype(f32)
        own = ends + pltpu.roll(ends, N1, 1)
        if block:
            missing.append(own * pltpu.roll(given, 4, 0) + given * pltpu.roll(own + given, 4, 0))
        given = pltpu.roll(own, N2 - 2, 1)
    return missing


def wave_at(device):
    row = lax.broadcasted_iota(jnp.int32, (8, N2), 0)
    k = 4 * device + row % 4 + N1 * lane_index((8, N2))
    angle = (k.astype(f32) + 0.25) * (-2.0 * math.pi / BLOCK)
    return jnp.where(row < 4, jnp.cos(angle), jnp.sin(angle))


def mix_kernel(in_ref, out_ref):
    top = lax.broadcasted_iota(jnp.int32, (8, N2), 0) < 4
    missing = edge_terms(in_ref)
    wave = wave_at(slot(lax.axis_index("seq"), OUT))
    for pair in range(2):
        sums = []
        for side in range(2):
            row = 2 * pair + side
            data, filt = [], []
            for block in range(SLICES):
                both = in_ref[slot(block, OUT), 16 * pair : 16 * pair + 16, :].astype(f32)
                tile = both[8 * side : 8 * side + 8]
                if block:
                    lack = missing[block][row : row + 1]
                    tile = tile + jnp.where(top, lack[:, 0:1], 0.0) + lack[:, 1:2] * wave
                data.append(tile)
                both = in_ref[slot(block, OUT), 32 + 16 * pair : 48 + 16 * pair, :].astype(f32)
                filt.append(both[8 * side : 8 * side + 8])
            swapped = [pltpu.roll(tile, 4, 0) for tile in data]
            real_parts, imag_parts = [], []
            for m in range(SLICES):
                tile = filt[m]
                if m:
                    turned = pltpu.roll(filt[m - 1], 4, 0)
                    tile = tile + jnp.where(top, -turned, turned)
                turned = pltpu.roll(tile, 4, 0)
                real_parts.append(jnp.where(top, tile, turned))
                imag_parts.append(jnp.where(top, -turned, tile))
            row = []
            for d in range(SLICES):
                total = None
                for e in range(d + 1):
                    term = data[e] * real_parts[d - e] + swapped[e] * imag_parts[d - e]
                    total = term if total is None else total + term
                row.append(total)
            sums.append(row)
        for d in range(SLICES):
            out_ref[slot(d, BACK), 16 * pair : 16 * pair + 16, :] = jnp.concatenate([sums[0][d], sums[1][d]], axis=0).astype(bf16)


def inverse_kernel(in_ref, queries_ref, direct_ref, outer_ref, cos_ref, sin_ref, inner_ref, out_ref):
    turned = []
    for pair in range(2):
        both = [in_ref[slot(OUT[p], BACK), 16 * pair : 16 * pair + 16, :].astype(f32) for p in range(SLICES)]
        for side in range(2):
            tile = jnp.concatenate([part[8 * side : 8 * side + 8] for part in both], axis=0)
            tile = inner_stage(tile, inner_ref[...])
            turned.append(tile * cos_ref[...] - halves_swapped(tile) * sin_ref[...])
    high, low = split(jnp.concatenate(turned, axis=1))
    stacked = jnp.concatenate([high, low, high], axis=0)
    convolved = jnp.dot(outer_ref[...], stacked, preferred_element_type=f32)
    for c in range(4):
        gated = queries_ref[c] * (convolved[:, N2 * c : N2 * (c + 1)] + direct_ref[c])
        gated = gated.astype(bf16)
        for copy in range(out_ref.shape[0]):
            out_ref[copy, N1 * c : N1 * (c + 1), :] = gated


def project_kernel(own_ref, other_ref, weight_ref, out_hbm, out_ref, sems):
    lines = N1 // sems.shape[0]
    copies = []
    for part in range(sems.shape[0]):
        tokens = pl.ds(part * lines * N2, lines * N2)
        other = other_ref[:, :, part * lines : (part + 1) * lines, :]
        other = other.reshape(own_ref.shape[0], lines, N2).reshape(own_ref.shape[0], lines * N2)
        rows = jnp.concatenate([own_ref[:, tokens], other], axis=0)
        done = lax.dot_general(rows, weight_ref[...], (((0,), (0,)), ((), ())), preferred_element_type=f32)
        out_ref[tokens, :] = done.astype(bf16)
        copies.append(pltpu.make_async_copy(out_ref.at[tokens, :], out_hbm.at[tokens, :], sems.at[part]))
        copies[-1].start()
    for copy in copies:
        copy.wait()


vmem = pl.BlockSpec(memory_space=pltpu.VMEM)
smem = pl.BlockSpec(memory_space=pltpu.SMEM)
hbm = pl.BlockSpec(memory_space=pltpu.HBM)


def call(kernel, specs, shape, dtype, *operands, scratch=(), grant=32 << 20):
    if isinstance(shape, list):
        out_shape, out_specs = [jax.ShapeDtypeStruct(s, d) for s, d in zip(shape, dtype)], [vmem] * len(shape)
    else:
        out_shape, out_specs = jax.ShapeDtypeStruct(shape, dtype), vmem
    return pl.pallas_call(
        kernel,
        out_shape=out_shape,
        in_specs=specs,
        out_specs=out_specs,
        scratch_shapes=scratch,
        compiler_params=pltpu.CompilerParams(vmem_limit_bytes=grant),
        cost_estimate=pl.CostEstimate(flops=1 << 24, bytes_accessed=1 << 20, transcendentals=0),
    )(*operands)


def gated_copies(features, short_taps, long_filter, skip_gain, copies):
    forward_outer, inverse_outer, turn_cos, turn_sin, forward_inner, inverse_inner = map(jnp.asarray, tables())
    held = (features, short_taps, long_filter, forward_outer, turn_cos, turn_sin, forward_inner)
    held = [pltpu.with_memory_space_constraint(x, pltpu.HBM) for x in held]
    rows = pltpu.VMEM((8 * N1, N2), f32)
    spectra = call(
        forward_kernel,
        [hbm] * 7,
        (SLICES, 72, N2),
        bf16,
        *held,
        scratch=[pltpu.VMEM((2, 4, BLOCK), bf16)]
        + [pltpu.VMEM(x.shape, x.dtype) for x in held[1:]]
        + [pltpu.VMEM((4, N2), bf16), rows, pltpu.SemaphoreType.DMA((8,))],
    )
    spectra = over_seq(spectra, OUT)
    queries, direct = call(
        gate_kernel,
        [hbm, vmem, vmem, smem],
        [(4, N1, N2)] * 2,
        [f32] * 2,
        features,
        short_taps,
        spectra,
        skip_gain,
        scratch=[
            pltpu.VMEM(features.shape, bf16),
            rows,
            pltpu.SemaphoreType.DMA(()),
        ],
    )
    mixed = call(mix_kernel, [vmem], (SLICES, 32, N2), bf16, spectra)
    mixed = over_seq(mixed, BACK)
    return call(
        inverse_kernel,
        [vmem] * 7,
        (copies, 4 * N1, N2),
        bf16,
        mixed,
        queries,
        direct,
        inverse_outer,
        turn_cos,
        turn_sin,
        inverse_inner,
    )


def gather_groups(chips):
    return [[2 * chip + core for chip in CHIPS] for core in range(2)]


def shards(features, short_taps, long_filter, skip_gain, out_weight):
    chan = lax.axis_size("chan")
    chips = chan // 2
    groups = gather_groups(chips)
    sent = gated_copies(features, short_taps, long_filter, skip_gain, chips)
    own = lax.all_to_all(sent, "chan", 0, 0, tiled=True, axis_index_groups=groups)
    other = lax.ppermute(own, "chan", [(d, d ^ 1) for d in range(chan)])
    blocks = out_weight.reshape(chan, 4, N2)
    sides = [jnp.concatenate([blocks[d] for d in groups[g] + groups[1 - g]], axis=0) for g in range(2)]
    weight = jnp.where(lax.axis_index("chan") % 2 == 0, sides[0], sides[1])
    return pl.pallas_call(
        project_kernel,
        out_shape=jax.ShapeDtypeStruct((BLOCK, N2), bf16),
        in_specs=[vmem] * 3,
        out_specs=hbm,
        scratch_shapes=[pltpu.VMEM((BLOCK, N2), bf16), pltpu.SemaphoreType.DMA((8,))],
        compiler_params=pltpu.CompilerParams(vmem_limit_bytes=24 << 20),
        cost_estimate=pl.CostEstimate(flops=1 << 28, bytes_accessed=1 << 22, transcendentals=0),
    )(own.reshape(4 * chips, BLOCK), other.reshape(chips, 4, N1, N2), weight)


def solution(mesh):
    placed = (
        P(None, "chan", "seq"),
        P(None, "chan", None),
        P("chan", "seq"),
        P("chan"),
        P(None, "chan"),
    )
    return jax.shard_map(
        shards, mesh=mesh, in_specs=placed, out_specs=P("seq", "chan"), check_vma=False
    )
```

```python
import math

import jax
import jax.numpy as jnp
import ml_dtypes
import numpy as np
from jax import lax
from jax.experimental import pallas as pl
from jax.experimental.pallas import tpu as pltpu
from jax.sharding import PartitionSpec as P

N1, N2 = 64, 128
BLOCK = N1 * N2
SLICES = 16
OUT = [(j + 12) % SLICES for j in range(SLICES)]
BACK = [8, 0, 1, 15, 2, 14, 3, 13, 4, 12, 5, 11, 6, 10, 7, 9]
CHIPS = [(j + 14) % 16 for j in range(16)]
f32, bf16 = jnp.float32, jnp.bfloat16


def split_table(table):
    high = table.astype(ml_dtypes.bfloat16)
    low = (table - high.astype(np.float64)).astype(ml_dtypes.bfloat16)
    return high, low


def tables():
    row = np.arange(2 * N1)
    k1 = 4 * (row // 8) + row % 4
    imag = (row // 4) % 2 == 1
    n1, n2 = np.arange(N1), np.arange(N2)
    phase = 2 * math.pi * np.outer(k1 + 0.25, n1) / N1
    outer = np.where(imag[:, None], -np.sin(phase), np.cos(phase))
    oh, ol = split_table(outer)
    forward_outer = np.concatenate([oh, oh, ol], axis=1)
    ih, il = split_table(outer.T / BLOCK)
    inverse_outer = np.concatenate([ih, ih, il], axis=1)
    angle = 2 * math.pi * np.outer(k1 + 0.25, n2) / BLOCK
    turn_cos = np.cos(angle).astype(np.float32)
    turn_sin = np.where(imag[:, None], -np.sin(angle), np.sin(angle)).astype(np.float32)
    phase = 2 * math.pi * np.outer(n2, n2) / N2

    def inner(sign):
        high, low = split_table(np.concatenate([np.cos(phase), sign * np.sin(phase)], axis=1))
        return np.concatenate([high, high, low], axis=0)

    return forward_outer, inverse_outer, turn_cos, turn_sin, inner(-1.0), inner(1.0)


def halves_swapped(tile):
    rows = tile.shape[0]
    return pltpu.roll(tile.reshape(rows // 8, 8, N2), 4, 1).reshape(rows, N2)


def split(value):
    high = value.astype(bf16)
    return high, (value - high.astype(f32)).astype(bf16)


def imag_sign(rows):
    return jnp.where(lax.broadcasted_iota(jnp.int32, (rows, N2), 0) % 8 < 4, -1.0, 1.0).astype(f32)


def inner_stage(rows, table):
    high, low = split(rows)
    both = jnp.dot(jnp.concatenate([high, low, high], axis=1), table, preferred_element_type=f32)
    return both[:, :N2] + imag_sign(rows.shape[0]) * halves_swapped(both[:, N2:])


def lane_index(shape):
    return lax.broadcasted_iota(jnp.int32, shape, 1)


def short_filter(stream, taps, edge=None):
    total = taps[:, 0:1] * stream
    for lag in (1, 2):
        turned = pltpu.roll(stream, lag, 1)
        head = turned[:, :N2]
        before = jnp.zeros_like(head) if edge is None else pltpu.roll(edge, lag, 1)
        head = jnp.where(lane_index(head.shape) < lag, before, head)
        total = total + taps[:, lag : lag + 1] * jnp.concatenate([head, turned[:, N2:]], axis=1)
    return total


def to_blocks(upper, lower, rows_ref):
    both = jnp.concatenate([upper, lower], axis=0)
    for n1 in range(N1):
        rows_ref[8 * n1 : 8 * n1 + 8, :] = both[:, N2 * n1 : N2 * (n1 + 1)]
    return [rows_ref[pl.ds(s, N1, stride=8), :] for s in range(8)]


def block_ends(query, streams, taps_ref):
    lane = lane_index((8, N2))
    first = jnp.concatenate([stream[:, :N2] for stream in streams], axis=0)
    last = jnp.concatenate([stream[:, BLOCK - N2 :] for stream in streams], axis=0)
    query = jnp.concatenate([query] * 2, axis=0)
    taps = jnp.concatenate([taps_ref[1], taps_ref[2]], axis=0)
    own = taps[:, 0:1] * first + jnp.where(lane == 1, taps[:, 1:2] * pltpu.roll(first, 1, 1), 0.0)
    given = taps[:, 2:3] * last + jnp.where(lane == N2 - 2, taps[:, 1:2] * pltpu.roll(last, N2 - 1, 1), 0.0)
    exact = jnp.where(lane < 2, own, pltpu.roll(given, 4, 1))
    rest = exact - exact.astype(bf16).astype(f32)
    rest = jnp.where(lane < N1 + 4, pltpu.roll(rest, N1, 1), jnp.where(lane < N2 - 2, pltpu.roll(query, N2 - 2, 1), last))
    return jnp.where(lane < 4, exact, rest)


def forward_kernel(
    feat_hbm, taps_hbm, filt_hbm, outer_hbm, cos_hbm, sin_hbm, inner_hbm, out_ref,
    feat_ref, taps_ref, filt_ref, outer_ref, cos_ref, sin_ref, inner_ref, last_ref, rows_ref, sems,
):
    last = pl.ds(BLOCK - N2, N2)
    sources = (feat_hbm.at[1:3], filt_hbm, taps_hbm, feat_hbm.at[0, :, last], outer_hbm, inner_hbm, cos_hbm, sin_hbm)
    places = (feat_ref, filt_ref, taps_ref, last_ref, outer_ref, inner_ref, cos_ref, sin_ref)
    copies = [pltpu.make_async_copy(s, d, sems.at[n]) for n, (s, d) in enumerate(zip(sources, places))]
    for copy in copies:
        copy.start()
    for copy in copies[:4]:
        copy.wait()
    streams = [feat_ref[i].astype(f32) for i in range(2)]
    ends = block_ends(last_ref[...].astype(f32), streams, taps_ref)
    ends = jnp.concatenate([ends, jnp.zeros_like(ends)], axis=0).astype(bf16)
    for device in range(SLICES):
        out_ref[device, 64:80, :] = ends
    product = short_filter(streams[0], taps_ref[1]) * short_filter(streams[1], taps_ref[2])
    signals = to_blocks(product, filt_ref[...], rows_ref)
    high, low = split(jnp.concatenate(signals, axis=1))
    stacked = jnp.concatenate([high, low, high], axis=0)
    for copy in copies[4:]:
        copy.wait()
    first = jnp.dot(outer_ref[...], stacked, preferred_element_type=f32)
    for pair in range(4):
        done = []
        for s in (2 * pair, 2 * pair + 1):
            tile = first[:, N2 * s : N2 * (s + 1)]
            tile = tile * cos_ref[...] + halves_swapped(tile) * sin_ref[...]
            done.append(inner_stage(tile, inner_ref[...]).reshape(SLICES, 8, N2))
        out_ref[:, 16 * pair : 16 * pair + 16, :] = jnp.concatenate(done, axis=1).astype(bf16)


def gate_kernel(feat_hbm, taps_ref, spectra_ref, gain_ref, queries_ref, direct_ref, feat_ref, rows_ref, sem):
    copy = pltpu.make_async_copy(feat_hbm, feat_ref, sem)
    copy.start()
    device = lax.axis_index("seq")
    ends = spectra_ref[slot(jnp.maximum(device - 1, 0), OUT), 64:80, :].astype(f32)[:8]
    ends = jnp.where(device > 0, ends, 0.0)
    edges = [pltpu.roll(ends, 2, 1)[:4], ends[:4], ends[4:]]
    copy.wait()
    mixed = [short_filter(feat_ref[i].astype(f32), taps_ref[i], edges[i]) for i in range(3)]
    rows = to_blocks(mixed[0], mixed[1] * mixed[2], rows_ref)
    for c in range(4):
        queries_ref[c] = rows[c]
        direct_ref[c] = gain_ref[c] * rows[4 + c]


def slot(device, order):
    if isinstance(device, int):
        return order.index(device)
    return sum(jnp.where(device == z, j, 0) for j, z in enumerate(order))


def over_seq(value, order):
    return lax.all_to_all(value, "seq", 0, 0, tiled=True, axis_index_groups=[order])


def edge_terms(in_ref):
    missing, given = [None], None
    for block in range(SLICES):
        ends = in_ref[slot(block, OUT), 64:80, :].astype(f32)[:8]
        own = ends + pltpu.roll(ends, N1, 1)
        if block:
            missing.append(own * pltpu.roll(given, 4, 0) + given * pltpu.roll(own + given, 4, 0))
        given = pltpu.roll(own, N2 - 2, 1)
    return missing


def wave_at(device):
    row = lax.broadcasted_iota(jnp.int32, (8, N2), 0)
    k = 4 * device + row % 4 + N1 * lane_index((8, N2))
    angle = (k.astype(f32) + 0.25) * (-2.0 * math.pi / BLOCK)
    return jnp.where(row < 4, jnp.cos(angle), jnp.sin(angle))


def mix_kernel(in_ref, out_ref):
    top = lax.broadcasted_iota(jnp.int32, (8, N2), 0) < 4
    missing = edge_terms(in_ref)
    wave = wave_at(slot(lax.axis_index("seq"), OUT))
    for pair in range(2):
        sums = []
        for side in range(2):
            row = 2 * pair + side
            data, filt = [], []
            for block in range(SLICES):
                both = in_ref[slot(block, OUT), 16 * pair : 16 * pair + 16, :].astype(f32)
                tile = both[8 * side : 8 * side + 8]
                if block:
                    lack = missing[block][row : row + 1]
                    tile = tile + jnp.where(top, lack[:, 0:1], 0.0) + lack[:, 1:2] * wave
                data.append(tile)
                both = in_ref[slot(block, OUT), 32 + 16 * pair : 48 + 16 * pair, :].astype(f32)
                filt.append(both[8 * side : 8 * side + 8])
            swapped = [pltpu.roll(tile, 4, 0) for tile in data]
            filter_swapped = [pltpu.roll(tile, 4, 0) for tile in filt]
            real_parts, imag_parts = [], []
            for m in range(SLICES):
                tile, turned = filt[m], filter_swapped[m]
                if m:
                    last = filter_swapped[m - 1]
                    tile = tile + jnp.where(top, -last, last)
                    turned = turned + jnp.where(top, filt[m - 1], -filt[m - 1])
                real_parts.append(jnp.where(top, tile, turned))
                imag_parts.append(jnp.where(top, -turned, tile))
            row = []
            for d in range(SLICES):
                total = None
                for e in range(d + 1):
                    term = data[e] * real_parts[d - e] + swapped[e] * imag_parts[d - e]
                    total = term if total is None else total + term
                row.append(total)
            sums.append(row)
        for d in range(SLICES):
            out_ref[slot(d, BACK), 16 * pair : 16 * pair + 16, :] = jnp.concatenate([sums[0][d], sums[1][d]], axis=0).astype(bf16)


def inverse_kernel(in_ref, queries_ref, direct_ref, outer_ref, cos_ref, sin_ref, inner_ref, out_ref):
    turned = []
    for pair in range(2):
        both = [in_ref[slot(OUT[p], BACK), 16 * pair : 16 * pair + 16, :].astype(f32) for p in range(SLICES)]
        for side in range(2):
            tile = jnp.concatenate([part[8 * side : 8 * side + 8] for part in both], axis=0)
            tile = inner_stage(tile, inner_ref[...])
            turned.append(tile * cos_ref[...] - halves_swapped(tile) * sin_ref[...])
    high, low = split(jnp.concatenate(turned, axis=1))
    stacked = jnp.concatenate([high, low, high], axis=0)
    convolved = jnp.dot(outer_ref[...], stacked, preferred_element_type=f32)
    for c in range(4):
        gated = queries_ref[c] * (convolved[:, N2 * c : N2 * (c + 1)] + direct_ref[c])
        gated = gated.astype(bf16)
        for copy in range(out_ref.shape[0]):
            out_ref[copy, N1 * c : N1 * (c + 1), :] = gated


def project_kernel(own_ref, other_ref, weight_ref, out_hbm, out_ref, sems):
    lines = N1 // sems.shape[0]
    copies = []
    for part in range(sems.shape[0]):
        tokens = pl.ds(part * lines * N2, lines * N2)
        other = other_ref[:, :, part * lines : (part + 1) * lines, :]
        other = other.reshape(own_ref.shape[0], lines, N2).reshape(own_ref.shape[0], lines * N2)
        rows = jnp.concatenate([own_ref[:, tokens], other], axis=0)
        done = lax.dot_general(rows, weight_ref[...], (((0,), (0,)), ((), ())), preferred_element_type=f32)
        out_ref[tokens, :] = done.astype(bf16)
        copies.append(pltpu.make_async_copy(out_ref.at[tokens, :], out_hbm.at[tokens, :], sems.at[part]))
        copies[-1].start()
    for copy in copies:
        copy.wait()


vmem = pl.BlockSpec(memory_space=pltpu.VMEM)
smem = pl.BlockSpec(memory_space=pltpu.SMEM)
hbm = pl.BlockSpec(memory_space=pltpu.HBM)


def call(kernel, specs, shape, dtype, *operands, scratch=(), grant=32 << 20):
    if isinstance(shape, list):
        out_shape, out_specs = [jax.ShapeDtypeStruct(s, d) for s, d in zip(shape, dtype)], [vmem] * len(shape)
    else:
        out_shape, out_specs = jax.ShapeDtypeStruct(shape, dtype), vmem
    return pl.pallas_call(
        kernel,
        out_shape=out_shape,
        in_specs=specs,
        out_specs=out_specs,
        scratch_shapes=scratch,
        compiler_params=pltpu.CompilerParams(vmem_limit_bytes=grant),
        cost_estimate=pl.CostEstimate(flops=1 << 24, bytes_accessed=1 << 20, transcendentals=0),
    )(*operands)


def gated_copies(features, short_taps, long_filter, skip_gain, copies):
    forward_outer, inverse_outer, turn_cos, turn_sin, forward_inner, inverse_inner = map(jnp.asarray, tables())
    held = (features, short_taps, long_filter, forward_outer, turn_cos, turn_sin, forward_inner)
    held = [pltpu.with_memory_space_constraint(x, pltpu.HBM) for x in held]
    rows = pltpu.VMEM((8 * N1, N2), f32)
    spectra = call(
        forward_kernel,
        [hbm] * 7,
        (SLICES, 80, N2),
        bf16,
        *held,
        scratch=[pltpu.VMEM((2, 4, BLOCK), bf16)]
        + [pltpu.VMEM(x.shape, x.dtype) for x in held[1:]]
        + [pltpu.VMEM((4, N2), bf16), rows, pltpu.SemaphoreType.DMA((8,))],
    )
    spectra = over_seq(spectra, OUT)
    queries, direct = call(
        gate_kernel,
        [hbm, vmem, vmem, smem],
        [(4, N1, N2)] * 2,
        [f32] * 2,
        features,
        short_taps,
        spectra,
        skip_gain,
        scratch=[
            pltpu.VMEM(features.shape, bf16),
            rows,
            pltpu.SemaphoreType.DMA(()),
        ],
    )
    mixed = call(mix_kernel, [vmem], (SLICES, 32, N2), bf16, spectra)
    mixed = over_seq(mixed, BACK)
    return call(
        inverse_kernel,
        [vmem] * 7,
        (copies, 4 * N1, N2),
        bf16,
        mixed,
        queries,
        direct,
        inverse_outer,
        turn_cos,
        turn_sin,
        inverse_inner,
    )


def gather_groups(chips):
    return [[2 * chip + core for chip in CHIPS] for core in range(2)]


def shards(features, short_taps, long_filter, skip_gain, out_weight):
    chan = lax.axis_size("chan")
    chips = chan // 2
    groups = gather_groups(chips)
    sent = gated_copies(features, short_taps, long_filter, skip_gain, chips)
    own = lax.all_to_all(sent, "chan", 0, 0, tiled=True, axis_index_groups=groups)
    other = lax.ppermute(own, "chan", [(d, d ^ 1) for d in range(chan)])
    blocks = out_weight.reshape(chan, 4, N2)
    sides = [jnp.concatenate([blocks[d] for d in groups[g] + groups[1 - g]], axis=0) for g in range(2)]
    weight = jnp.where(lax.axis_index("chan") % 2 == 0, sides[0], sides[1])
    return pl.pallas_call(
        project_kernel,
        out_shape=jax.ShapeDtypeStruct((BLOCK, N2), bf16),
        in_specs=[vmem] * 3,
        out_specs=hbm,
        scratch_shapes=[pltpu.VMEM((BLOCK, N2), bf16), pltpu.SemaphoreType.DMA((8,))],
        compiler_params=pltpu.CompilerParams(vmem_limit_bytes=24 << 20),
        cost_estimate=pl.CostEstimate(flops=1 << 28, bytes_accessed=1 << 22, transcendentals=0),
    )(own.reshape(4 * chips, BLOCK), other.reshape(chips, 4, N1, N2), weight)


def solution(mesh):
    placed = (
        P(None, "chan", "seq"),
        P(None, "chan", None),
        P("chan", "seq"),
        P("chan"),
        P(None, "chan"),
    )
    return jax.shard_map(
        shards, mesh=mesh, in_specs=placed, out_specs=P("seq", "chan"), check_vma=False
    )
```

```python
import math

import jax
import jax.numpy as jnp
import ml_dtypes
import numpy as np
from jax import lax
from jax.experimental import pallas as pl
from jax.experimental.pallas import tpu as pltpu
from jax.sharding import PartitionSpec as P

N1, N2 = 64, 128
BLOCK = N1 * N2
SLICES = 16
OUT = [(j + 12) % SLICES for j in range(SLICES)]
BACK = [8, 0, 1, 15, 2, 14, 3, 13, 4, 12, 5, 11, 6, 10, 7, 9]
CHIPS = [(j + 14) % 16 for j in range(16)]
f32, bf16 = jnp.float32, jnp.bfloat16


def split_table(table):
    high = table.astype(ml_dtypes.bfloat16)
    low = (table - high.astype(np.float64)).astype(ml_dtypes.bfloat16)
    return high, low


def tables():
    row = np.arange(2 * N1)
    k1 = 4 * (row // 8) + row % 4
    imag = (row // 4) % 2 == 1
    n1, n2 = np.arange(N1), np.arange(N2)
    phase = 2 * math.pi * np.outer(k1 + 0.25, n1) / N1
    outer = np.where(imag[:, None], -np.sin(phase), np.cos(phase))
    oh, ol = split_table(outer)
    forward_outer = np.concatenate([oh, oh, ol], axis=1)
    ih, il = split_table(outer.T / BLOCK)
    inverse_outer = np.concatenate([ih, ih, il], axis=1)
    angle = 2 * math.pi * np.outer(k1 + 0.25, n2) / BLOCK
    turn_cos = np.cos(angle).astype(np.float32)
    turn_sin = np.where(imag[:, None], -np.sin(angle), np.sin(angle)).astype(np.float32)
    phase = 2 * math.pi * np.outer(n2, n2) / N2

    def inner(sign):
        high, low = split_table(np.concatenate([np.cos(phase), sign * np.sin(phase)], axis=1))
        return np.concatenate([high, low], axis=0)

    return forward_outer, inverse_outer, turn_cos, turn_sin, inner(-1.0), inner(1.0)


def halves_swapped(tile):
    rows = tile.shape[0]
    return pltpu.roll(tile.reshape(rows // 8, 8, N2), 4, 1).reshape(rows, N2)


def split(value):
    high = value.astype(bf16)
    return high, (value - high.astype(f32)).astype(bf16)


def imag_sign(rows):
    return jnp.where(lax.broadcasted_iota(jnp.int32, (rows, N2), 0) % 8 < 4, -1.0, 1.0).astype(f32)


def inner_stage(rows, table):
    high, low = split(rows)
    table = jnp.concatenate([table[:N2], table], axis=0)
    both = jnp.dot(jnp.concatenate([high, low, high], axis=1), table, preferred_element_type=f32)
    return both[:, :N2] + imag_sign(rows.shape[0]) * halves_swapped(both[:, N2:])


def lane_index(shape):
    return lax.broadcasted_iota(jnp.int32, shape, 1)


def short_filter(stream, taps, edge=None):
    total = taps[:, 0:1] * stream
    for lag in (1, 2):
        turned = pltpu.roll(stream, lag, 1)
        head = turned[:, :N2]
        before = jnp.zeros_like(head) if edge is None else pltpu.roll(edge, lag, 1)
        head = jnp.where(lane_index(head.shape) < lag, before, head)
        total = total + taps[:, lag : lag + 1] * jnp.concatenate([head, turned[:, N2:]], axis=1)
    return total


def to_blocks(upper, lower, rows_ref):
    both = jnp.concatenate([upper, lower], axis=0)
    for n1 in range(N1):
        rows_ref[8 * n1 : 8 * n1 + 8, :] = both[:, N2 * n1 : N2 * (n1 + 1)]
    return [rows_ref[pl.ds(s, N1, stride=8), :] for s in range(8)]


def block_ends(query, streams, taps_ref):
    lane = lane_index((8, N2))
    first = jnp.concatenate([stream[:, :N2] for stream in streams], axis=0)
    last = jnp.concatenate([stream[:, BLOCK - N2 :] for stream in streams], axis=0)
    query = jnp.concatenate([query] * 2, axis=0)
    taps = jnp.concatenate([taps_ref[1], taps_ref[2]], axis=0)
    own = taps[:, 0:1] * first + jnp.where(lane == 1, taps[:, 1:2] * pltpu.roll(first, 1, 1), 0.0)
    given = taps[:, 2:3] * last + jnp.where(lane == N2 - 2, taps[:, 1:2] * pltpu.roll(last, N2 - 1, 1), 0.0)
    exact = jnp.where(lane < 2, own, pltpu.roll(given, 4, 1))
    rest = exact - exact.astype(bf16).astype(f32)
    rest = jnp.where(lane < N1 + 4, pltpu.roll(rest, N1, 1), jnp.where(lane < N2 - 2, pltpu.roll(query, N2 - 2, 1), last))
    return jnp.where(lane < 4, exact, rest)


def forward_kernel(
    feat_hbm, taps_hbm, filt_hbm, outer_hbm, cos_hbm, sin_hbm, inner_hbm, out_ref,
    feat_ref, taps_ref, filt_ref, outer_ref, cos_ref, sin_ref, inner_ref, last_ref, rows_ref, sems,
):
    last = pl.ds(BLOCK - N2, N2)
    sources = (feat_hbm.at[1:3], filt_hbm, taps_hbm, feat_hbm.at[0, :, last], outer_hbm, inner_hbm, cos_hbm, sin_hbm)
    places = (feat_ref, filt_ref, taps_ref, last_ref, outer_ref, inner_ref, cos_ref, sin_ref)
    copies = [pltpu.make_async_copy(s, d, sems.at[n]) for n, (s, d) in enumerate(zip(sources, places))]
    for copy in copies:
        copy.start()
    for copy in copies[:4]:
        copy.wait()
    streams = [feat_ref[i].astype(f32) for i in range(2)]
    ends = block_ends(last_ref[...].astype(f32), streams, taps_ref).astype(bf16)
    for device in range(SLICES):
        out_ref[device, 64:72, :] = ends
    product = short_filter(streams[0], taps_ref[1]) * short_filter(streams[1], taps_ref[2])
    signals = to_blocks(product, filt_ref[...], rows_ref)
    high, low = split(jnp.concatenate(signals, axis=1))
    stacked = jnp.concatenate([high, low, high], axis=0)
    for copy in copies[4:]:
        copy.wait()
    first = jnp.dot(outer_ref[...], stacked, preferred_element_type=f32)
    for pair in range(4):
        done = []
        for s in (2 * pair, 2 * pair + 1):
            tile = first[:, N2 * s : N2 * (s + 1)]
            tile = tile * cos_ref[...] + halves_swapped(tile) * sin_ref[...]
            done.append(inner_stage(tile, inner_ref[...]).reshape(SLICES, 8, N2))
        out_ref[:, 16 * pair : 16 * pair + 16, :] = jnp.concatenate(done, axis=1).astype(bf16)


def gate_kernel(feat_hbm, taps_ref, spectra_ref, gain_ref, queries_ref, direct_ref, feat_ref, rows_ref, sem):
    copy = pltpu.make_async_copy(feat_hbm, feat_ref, sem)
    copy.start()
    device = lax.axis_index("seq")
    ends = spectra_ref[slot(jnp.maximum(device - 1, 0), OUT), 64:72, :].astype(f32)
    ends = jnp.where(device > 0, ends, 0.0)
    edges = [pltpu.roll(ends, 2, 1)[:4], ends[:4], ends[4:]]
    copy.wait()
    mixed = [short_filter(feat_ref[i].astype(f32), taps_ref[i], edges[i]) for i in range(3)]
    rows = to_blocks(mixed[0], mixed[1] * mixed[2], rows_ref)
    for c in range(4):
        queries_ref[c] = rows[c]
        direct_ref[c] = gain_ref[c] * rows[4 + c]


def slot(device, order):
    if isinstance(device, int):
        return order.index(device)
    return sum(jnp.where(device == z, j, 0) for j, z in enumerate(order))


def over_seq(value, order):
    return lax.all_to_all(value, "seq", 0, 0, tiled=True, axis_index_groups=[order])


def edge_terms(in_ref):
    missing, given = [None], None
    for block in range(SLICES):
        ends = in_ref[slot(block, OUT), 64:72, :].astype(f32)
        own = ends + pltpu.roll(ends, N1, 1)
        if block:
            missing.append(own * pltpu.roll(given, 4, 0) + given * pltpu.roll(own + given, 4, 0))
        given = pltpu.roll(own, N2 - 2, 1)
    return missing


def wave_at(device):
    row = lax.broadcasted_iota(jnp.int32, (8, N2), 0)
    k = 4 * device + row % 4 + N1 * lane_index((8, N2))
    angle = (k.astype(f32) + 0.25) * (-2.0 * math.pi / BLOCK)
    return jnp.where(row < 4, jnp.cos(angle), jnp.sin(angle))


def mix_kernel(in_ref, out_ref):
    top = lax.broadcasted_iota(jnp.int32, (8, N2), 0) < 4
    missing = edge_terms(in_ref)
    wave = wave_at(slot(lax.axis_index("seq"), OUT))
    for pair in range(2):
        sums = []
        for side in range(2):
            row = 2 * pair + side
            data, filt = [], []
            for block in range(SLICES):
                both = in_ref[slot(block, OUT), 16 * pair : 16 * pair + 16, :].astype(f32)
                tile = both[8 * side : 8 * side + 8]
                if block:
                    lack = missing[block][row : row + 1]
                    tile = tile + jnp.where(top, lack[:, 0:1], 0.0) + lack[:, 1:2] * wave
                data.append(tile)
                both = in_ref[slot(block, OUT), 32 + 16 * pair : 48 + 16 * pair, :].astype(f32)
                filt.append(both[8 * side : 8 * side + 8])
            swapped = [pltpu.roll(tile, 4, 0) for tile in data]
            filter_swapped = [pltpu.roll(tile, 4, 0) for tile in filt]
            real_parts, imag_parts = [], []
            for m in range(SLICES):
                tile, turned = filt[m], filter_swapped[m]
                if m:
                    last = filter_swapped[m - 1]
                    tile = tile + jnp.where(top, -last, last)
                    turned = turned + jnp.where(top, filt[m - 1], -filt[m - 1])
                real_parts.append(jnp.where(top, tile, turned))
                imag_parts.append(jnp.where(top, -turned, tile))
            row = []
            for d in range(SLICES):
                total = None
                for e in range(d + 1):
                    term = data[e] * real_parts[d - e] + swapped[e] * imag_parts[d - e]
                    total = term if total is None else total + term
                row.append(total)
            sums.append(row)
        for d in range(SLICES):
            out_ref[slot(d, BACK), 16 * pair : 16 * pair + 16, :] = jnp.concatenate([sums[0][d], sums[1][d]], axis=0).astype(bf16)


def inverse_kernel(in_ref, queries_ref, direct_ref, outer_ref, cos_ref, sin_ref, inner_ref, out_ref):
    turned = []
    for pair in range(2):
        both = [in_ref[slot(OUT[p], BACK), 16 * pair : 16 * pair + 16, :].astype(f32) for p in range(SLICES)]
        for side in range(2):
            tile = jnp.concatenate([part[8 * side : 8 * side + 8] for part in both], axis=0)
            tile = inner_stage(tile, inner_ref[...])
            turned.append(tile * cos_ref[...] - halves_swapped(tile) * sin_ref[...])
    high, low = split(jnp.concatenate(turned, axis=1))
    stacked = jnp.concatenate([high, low, high], axis=0)
    convolved = jnp.dot(outer_ref[...], stacked, preferred_element_type=f32)
    for c in range(4):
        gated = queries_ref[c] * (convolved[:, N2 * c : N2 * (c + 1)] + direct_ref[c])
        gated = gated.astype(bf16)
        for copy in range(out_ref.shape[0]):
            out_ref[copy, N1 * c : N1 * (c + 1), :] = gated


def project_kernel(own_ref, other_ref, weight_ref, out_hbm, out_ref, sems):
    lines = N1 // sems.shape[0]
    copies = []
    for part in range(sems.shape[0]):
        tokens = pl.ds(part * lines * N2, lines * N2)
        other = other_ref[:, :, part * lines : (part + 1) * lines, :]
        other = other.reshape(own_ref.shape[0], lines, N2).reshape(own_ref.shape[0], lines * N2)
        rows = jnp.concatenate([own_ref[:, tokens], other], axis=0)
        done = lax.dot_general(rows, weight_ref[...], (((0,), (0,)), ((), ())), preferred_element_type=f32)
        out_ref[tokens, :] = done.astype(bf16)
        copies.append(pltpu.make_async_copy(out_ref.at[tokens, :], out_hbm.at[tokens, :], sems.at[part]))
        copies[-1].start()
    for copy in copies:
        copy.wait()


vmem = pl.BlockSpec(memory_space=pltpu.VMEM)
smem = pl.BlockSpec(memory_space=pltpu.SMEM)
hbm = pl.BlockSpec(memory_space=pltpu.HBM)


def call(kernel, specs, shape, dtype, *operands, scratch=(), grant=32 << 20):
    if isinstance(shape, list):
        out_shape, out_specs = [jax.ShapeDtypeStruct(s, d) for s, d in zip(shape, dtype)], [vmem] * len(shape)
    else:
        out_shape, out_specs = jax.ShapeDtypeStruct(shape, dtype), vmem
    return pl.pallas_call(
        kernel,
        out_shape=out_shape,
        in_specs=specs,
        out_specs=out_specs,
        scratch_shapes=scratch,
        compiler_params=pltpu.CompilerParams(vmem_limit_bytes=grant),
        cost_estimate=pl.CostEstimate(flops=1 << 24, bytes_accessed=1 << 20, transcendentals=0),
    )(*operands)


def gated_copies(features, short_taps, long_filter, skip_gain, copies):
    forward_outer, inverse_outer, turn_cos, turn_sin, forward_inner, inverse_inner = map(jnp.asarray, tables())
    held = (features, short_taps, long_filter, forward_outer, turn_cos, turn_sin, forward_inner)
    held = [pltpu.with_memory_space_constraint(x, pltpu.HBM) for x in held]
    rows = pltpu.VMEM((8 * N1, N2), f32)
    spectra = call(
        forward_kernel,
        [hbm] * 7,
        (SLICES, 72, N2),
        bf16,
        *held,
        scratch=[pltpu.VMEM((2, 4, BLOCK), bf16)]
        + [pltpu.VMEM(x.shape, x.dtype) for x in held[1:]]
        + [pltpu.VMEM((4, N2), bf16), rows, pltpu.SemaphoreType.DMA((8,))],
    )
    spectra = over_seq(spectra, OUT)
    queries, direct = call(
        gate_kernel,
        [hbm, vmem, vmem, smem],
        [(4, N1, N2)] * 2,
        [f32] * 2,
        features,
        short_taps,
        spectra,
        skip_gain,
        scratch=[
            pltpu.VMEM(features.shape, bf16),
            rows,
            pltpu.SemaphoreType.DMA(()),
        ],
    )
    mixed = call(mix_kernel, [vmem], (SLICES, 32, N2), bf16, spectra)
    mixed = over_seq(mixed, BACK)
    return call(
        inverse_kernel,
        [vmem] * 7,
        (copies, 4 * N1, N2),
        bf16,
        mixed,
        queries,
        direct,
        inverse_outer,
        turn_cos,
        turn_sin,
        inverse_inner,
    )


def gather_groups(chips):
    return [[2 * chip + core for chip in CHIPS] for core in range(2)]


def shards(features, short_taps, long_filter, skip_gain, out_weight):
    chan = lax.axis_size("chan")
    chips = chan // 2
    groups = gather_groups(chips)
    sent = gated_copies(features, short_taps, long_filter, skip_gain, chips)
    own = lax.all_to_all(sent, "chan", 0, 0, tiled=True, axis_index_groups=groups)
    other = lax.ppermute(own, "chan", [(d, d ^ 1) for d in range(chan)])
    blocks = out_weight.reshape(chan, 4, N2)
    sides = [jnp.concatenate([blocks[d] for d in groups[g] + groups[1 - g]], axis=0) for g in range(2)]
    weight = jnp.where(lax.axis_index("chan") % 2 == 0, sides[0], sides[1])
    return pl.pallas_call(
        project_kernel,
        out_shape=jax.ShapeDtypeStruct((BLOCK, N2), bf16),
        in_specs=[vmem] * 3,
        out_specs=hbm,
        scratch_shapes=[pltpu.VMEM((BLOCK, N2), bf16), pltpu.SemaphoreType.DMA((8,))],
        compiler_params=pltpu.CompilerParams(vmem_limit_bytes=24 << 20),
        cost_estimate=pl.CostEstimate(flops=1 << 28, bytes_accessed=1 << 22, transcendentals=0),
    )(own.reshape(4 * chips, BLOCK), other.reshape(chips, 4, N1, N2), weight)


def solution(mesh):
    placed = (
        P(None, "chan", "seq"),
        P(None, "chan", None),
        P("chan", "seq"),
        P("chan"),
        P(None, "chan"),
    )
    return jax.shard_map(
        shards, mesh=mesh, in_specs=placed, out_specs=P("seq", "chan"), check_vma=False
    )
```

```python
import math

import jax
import jax.numpy as jnp
import ml_dtypes
import numpy as np
from jax import lax
from jax.experimental import pallas as pl
from jax.experimental.pallas import tpu as pltpu
from jax.sharding import PartitionSpec as P

N1, N2 = 64, 128
BLOCK = N1 * N2
SLICES = 16
OUT = [(j + 10) % SLICES for j in range(SLICES)]
BACK = [8, 0, 1, 15, 2, 14, 3, 13, 4, 12, 5, 11, 6, 10, 7, 9]
CHIPS = [(j + 14) % 16 for j in range(16)]
f32, bf16 = jnp.float32, jnp.bfloat16


def split_table(table):
    high = table.astype(ml_dtypes.bfloat16)
    low = (table - high.astype(np.float64)).astype(ml_dtypes.bfloat16)
    return high, low


def tables():
    row = np.arange(2 * N1)
    k1 = 4 * (row // 8) + row % 4
    imag = (row // 4) % 2 == 1
    n1, n2 = np.arange(N1), np.arange(N2)
    phase = 2 * math.pi * np.outer(k1 + 0.25, n1) / N1
    outer = np.where(imag[:, None], -np.sin(phase), np.cos(phase))
    oh, ol = split_table(outer)
    forward_outer = np.concatenate([oh, oh, ol], axis=1)
    ih, il = split_table(outer.T / BLOCK)
    inverse_outer = np.concatenate([ih, ih, il], axis=1)
    angle = 2 * math.pi * np.outer(k1 + 0.25, n2) / BLOCK
    turn_cos = np.cos(angle).astype(np.float32)
    turn_sin = np.where(imag[:, None], -np.sin(angle), np.sin(angle)).astype(np.float32)
    phase = 2 * math.pi * np.outer(n2, n2) / N2

    def inner(sign):
        high, low = split_table(np.concatenate([np.cos(phase), sign * np.sin(phase)], axis=1))
        return np.concatenate([high, low], axis=0)

    return forward_outer, inverse_outer, turn_cos, turn_sin, inner(-1.0), inner(1.0)


def halves_swapped(tile):
    rows = tile.shape[0]
    return pltpu.roll(tile.reshape(rows // 8, 8, N2), 4, 1).reshape(rows, N2)


def split(value):
    high = value.astype(bf16)
    return high, (value - high.astype(f32)).astype(bf16)


def imag_sign(rows):
    return jnp.where(lax.broadcasted_iota(jnp.int32, (rows, N2), 0) % 8 < 4, -1.0, 1.0).astype(f32)


def inner_stage(rows, table):
    high, low = split(rows)
    table = jnp.concatenate([table[:N2], table], axis=0)
    both = jnp.dot(jnp.concatenate([high, low, high], axis=1), table, preferred_element_type=f32)
    return both[:, :N2] + imag_sign(rows.shape[0]) * halves_swapped(both[:, N2:])


def lane_index(shape):
    return lax.broadcasted_iota(jnp.int32, shape, 1)


def short_filter(stream, taps, edge=None):
    total = taps[:, 0:1] * stream
    for lag in (1, 2):
        turned = pltpu.roll(stream, lag, 1)
        head = turned[:, :N2]
        before = jnp.zeros_like(head) if edge is None else pltpu.roll(edge, lag, 1)
        head = jnp.where(lane_index(head.shape) < lag, before, head)
        total = total + taps[:, lag : lag + 1] * jnp.concatenate([head, turned[:, N2:]], axis=1)
    return total


def to_blocks(upper, lower, rows_ref):
    both = jnp.concatenate([upper, lower], axis=0)
    for n1 in range(N1):
        rows_ref[8 * n1 : 8 * n1 + 8, :] = both[:, N2 * n1 : N2 * (n1 + 1)]
    return [rows_ref[pl.ds(s, N1, stride=8), :] for s in range(8)]


def block_ends(query, streams, taps_ref):
    lane = lane_index((8, N2))
    first = jnp.concatenate([stream[:, :N2] for stream in streams], axis=0)
    last = jnp.concatenate([stream[:, BLOCK - N2 :] for stream in streams], axis=0)
    query = jnp.concatenate([query] * 2, axis=0)
    taps = jnp.concatenate([taps_ref[1], taps_ref[2]], axis=0)
    own = taps[:, 0:1] * first + jnp.where(lane == 1, taps[:, 1:2] * pltpu.roll(first, 1, 1), 0.0)
    given = taps[:, 2:3] * last + jnp.where(lane == N2 - 2, taps[:, 1:2] * pltpu.roll(last, N2 - 1, 1), 0.0)
    exact = jnp.where(lane < 2, own, pltpu.roll(given, 4, 1))
    rest = exact - exact.astype(bf16).astype(f32)
    rest = jnp.where(lane < N1 + 4, pltpu.roll(rest, N1, 1), jnp.where(lane < N2 - 2, pltpu.roll(query, N2 - 2, 1), last))
    return jnp.where(lane < 4, exact, rest)


def forward_kernel(
    feat_hbm, taps_hbm, filt_hbm, outer_hbm, cos_hbm, sin_hbm, inner_hbm, out_ref,
    feat_ref, taps_ref, filt_ref, outer_ref, cos_ref, sin_ref, inner_ref, last_ref, rows_ref, sems,
):
    last = pl.ds(BLOCK - N2, N2)
    sources = (feat_hbm.at[1:3], filt_hbm, taps_hbm, feat_hbm.at[0, :, last], outer_hbm, inner_hbm, cos_hbm, sin_hbm)
    places = (feat_ref, filt_ref, taps_ref, last_ref, outer_ref, inner_ref, cos_ref, sin_ref)
    copies = [pltpu.make_async_copy(s, d, sems.at[n]) for n, (s, d) in enumerate(zip(sources, places))]
    for copy in copies:
        copy.start()
    for copy in copies[:4]:
        copy.wait()
    streams = [feat_ref[i].astype(f32) for i in range(2)]
    ends = block_ends(last_ref[...].astype(f32), streams, taps_ref).astype(bf16)
    for device in range(SLICES):
        out_ref[device, 64:72, :] = ends
    product = short_filter(streams[0], taps_ref[1]) * short_filter(streams[1], taps_ref[2])
    signals = to_blocks(product, filt_ref[...], rows_ref)
    high, low = split(jnp.concatenate(signals, axis=1))
    stacked = jnp.concatenate([high, low, high], axis=0)
    for copy in copies[4:]:
        copy.wait()
    first = jnp.dot(outer_ref[...], stacked, preferred_element_type=f32)
    for pair in range(4):
        done = []
        for s in (2 * pair, 2 * pair + 1):
            tile = first[:, N2 * s : N2 * (s + 1)]
            tile = tile * cos_ref[...] + halves_swapped(tile) * sin_ref[...]
            done.append(inner_stage(tile, inner_ref[...]).reshape(SLICES, 8, N2))
        out_ref[:, 16 * pair : 16 * pair + 16, :] = jnp.concatenate(done, axis=1).astype(bf16)


def gate_kernel(feat_hbm, taps_ref, spectra_ref, gain_ref, queries_ref, direct_ref, feat_ref, rows_ref, sem):
    copy = pltpu.make_async_copy(feat_hbm, feat_ref, sem)
    copy.start()
    device = lax.axis_index("seq")
    ends = spectra_ref[slot(jnp.maximum(device - 1, 0), OUT), 64:72, :].astype(f32)
    ends = jnp.where(device > 0, ends, 0.0)
    edges = [pltpu.roll(ends, 2, 1)[:4], ends[:4], ends[4:]]
    copy.wait()
    mixed = [short_filter(feat_ref[i].astype(f32), taps_ref[i], edges[i]) for i in range(3)]
    rows = to_blocks(mixed[0], mixed[1] * mixed[2], rows_ref)
    for c in range(4):
        queries_ref[c] = rows[c]
        direct_ref[c] = gain_ref[c] * rows[4 + c]


def slot(device, order):
    if isinstance(device, int):
        return order.index(device)
    return sum(jnp.where(device == z, j, 0) for j, z in enumerate(order))


def over_seq(value, order):
    return lax.all_to_all(value, "seq", 0, 0, tiled=True, axis_index_groups=[order])


def edge_terms(in_ref):
    missing, given = [None], None
    for block in range(SLICES):
        ends = in_ref[slot(block, OUT), 64:72, :].astype(f32)
        own = ends + pltpu.roll(ends, N1, 1)
        if block:
            missing.append(own * pltpu.roll(given, 4, 0) + given * pltpu.roll(own + given, 4, 0))
        given = pltpu.roll(own, N2 - 2, 1)
    return missing


def wave_at(device):
    row = lax.broadcasted_iota(jnp.int32, (8, N2), 0)
    k = 4 * device + row % 4 + N1 * lane_index((8, N2))
    angle = (k.astype(f32) + 0.25) * (-2.0 * math.pi / BLOCK)
    return jnp.where(row < 4, jnp.cos(angle), jnp.sin(angle))


def mix_kernel(in_ref, out_ref):
    top = lax.broadcasted_iota(jnp.int32, (8, N2), 0) < 4
    missing = edge_terms(in_ref)
    wave = wave_at(slot(lax.axis_index("seq"), OUT))
    for pair in range(2):
        sums = []
        for side in range(2):
            row = 2 * pair + side
            data, filt = [], []
            for block in range(SLICES):
                both = in_ref[slot(block, OUT), 16 * pair : 16 * pair + 16, :].astype(f32)
                tile = both[8 * side : 8 * side + 8]
                if block:
                    lack = missing[block][row : row + 1]
                    tile = tile + jnp.where(top, lack[:, 0:1], 0.0) + lack[:, 1:2] * wave
                data.append(tile)
                both = in_ref[slot(block, OUT), 32 + 16 * pair : 48 + 16 * pair, :].astype(f32)
                filt.append(both[8 * side : 8 * side + 8])
            swapped = [pltpu.roll(tile, 4, 0) for tile in data]
            filter_swapped = [pltpu.roll(tile, 4, 0) for tile in filt]
            real_parts, imag_parts = [], []
            for m in range(SLICES):
                tile, turned = filt[m], filter_swapped[m]
                if m:
                    last = filter_swapped[m - 1]
                    tile = tile + jnp.where(top, -last, last)
                    turned = turned + jnp.where(top, filt[m - 1], -filt[m - 1])
                real_parts.append(jnp.where(top, tile, turned))
                imag_parts.append(jnp.where(top, -turned, tile))
            row = []
            for d in range(SLICES):
                total = None
                for e in range(d + 1):
                    term = data[e] * real_parts[d - e] + swapped[e] * imag_parts[d - e]
                    total = term if total is None else total + term
                row.append(total)
            sums.append(row)
        for d in range(SLICES):
            out_ref[slot(d, BACK), 16 * pair : 16 * pair + 16, :] = jnp.concatenate([sums[0][d], sums[1][d]], axis=0).astype(bf16)


def inverse_kernel(in_ref, queries_ref, direct_ref, outer_ref, cos_ref, sin_ref, inner_ref, out_ref):
    turned = []
    for pair in range(2):
        both = [in_ref[slot(OUT[p], BACK), 16 * pair : 16 * pair + 16, :].astype(f32) for p in range(SLICES)]
        for side in range(2):
            tile = jnp.concatenate([part[8 * side : 8 * side + 8] for part in both], axis=0)
            tile = inner_stage(tile, inner_ref[...])
            turned.append(tile * cos_ref[...] - halves_swapped(tile) * sin_ref[...])
    high, low = split(jnp.concatenate(turned, axis=1))
    stacked = jnp.concatenate([high, low, high], axis=0)
    convolved = jnp.dot(outer_ref[...], stacked, preferred_element_type=f32)
    for c in range(4):
        gated = queries_ref[c] * (convolved[:, N2 * c : N2 * (c + 1)] + direct_ref[c])
        gated = gated.astype(bf16)
        for copy in range(out_ref.shape[0]):
            out_ref[copy, N1 * c : N1 * (c + 1), :] = gated


def project_kernel(own_ref, other_ref, weight_ref, out_hbm, out_ref, sems):
    lines = N1 // sems.shape[0]
    copies = []
    for part in range(sems.shape[0]):
        tokens = pl.ds(part * lines * N2, lines * N2)
        other = other_ref[:, :, part * lines : (part + 1) * lines, :]
        other = other.reshape(own_ref.shape[0], lines, N2).reshape(own_ref.shape[0], lines * N2)
        rows = jnp.concatenate([own_ref[:, tokens], other], axis=0)
        done = lax.dot_general(rows, weight_ref[...], (((0,), (0,)), ((), ())), preferred_element_type=f32)
        out_ref[tokens, :] = done.astype(bf16)
        copies.append(pltpu.make_async_copy(out_ref.at[tokens, :], out_hbm.at[tokens, :], sems.at[part]))
        copies[-1].start()
    for copy in copies:
        copy.wait()


vmem = pl.BlockSpec(memory_space=pltpu.VMEM)
smem = pl.BlockSpec(memory_space=pltpu.SMEM)
hbm = pl.BlockSpec(memory_space=pltpu.HBM)


def call(kernel, specs, shape, dtype, *operands, scratch=(), grant=32 << 20):
    if isinstance(shape, list):
        out_shape, out_specs = [jax.ShapeDtypeStruct(s, d) for s, d in zip(shape, dtype)], [vmem] * len(shape)
    else:
        out_shape, out_specs = jax.ShapeDtypeStruct(shape, dtype), vmem
    return pl.pallas_call(
        kernel,
        out_shape=out_shape,
        in_specs=specs,
        out_specs=out_specs,
        scratch_shapes=scratch,
        compiler_params=pltpu.CompilerParams(vmem_limit_bytes=grant),
        cost_estimate=pl.CostEstimate(flops=1 << 24, bytes_accessed=1 << 20, transcendentals=0),
    )(*operands)


def gated_copies(features, short_taps, long_filter, skip_gain, copies):
    forward_outer, inverse_outer, turn_cos, turn_sin, forward_inner, inverse_inner = map(jnp.asarray, tables())
    held = (features, short_taps, long_filter, forward_outer, turn_cos, turn_sin, forward_inner)
    held = [pltpu.with_memory_space_constraint(x, pltpu.HBM) for x in held]
    rows = pltpu.VMEM((8 * N1, N2), f32)
    spectra = call(
        forward_kernel,
        [hbm] * 7,
        (SLICES, 72, N2),
        bf16,
        *held,
        scratch=[pltpu.VMEM((2, 4, BLOCK), bf16)]
        + [pltpu.VMEM(x.shape, x.dtype) for x in held[1:]]
        + [pltpu.VMEM((4, N2), bf16), rows, pltpu.SemaphoreType.DMA((8,))],
    )
    spectra = over_seq(spectra, OUT)
    queries, direct = call(
        gate_kernel,
        [hbm, vmem, vmem, smem],
        [(4, N1, N2)] * 2,
        [f32] * 2,
        features,
        short_taps,
        spectra,
        skip_gain,
        scratch=[
            pltpu.VMEM(features.shape, bf16),
            rows,
            pltpu.SemaphoreType.DMA(()),
        ],
    )
    mixed = call(mix_kernel, [vmem], (SLICES, 32, N2), bf16, spectra)
    mixed = over_seq(mixed, BACK)
    return call(
        inverse_kernel,
        [vmem] * 7,
        (copies, 4 * N1, N2),
        bf16,
        mixed,
        queries,
        direct,
        inverse_outer,
        turn_cos,
        turn_sin,
        inverse_inner,
    )


def gather_groups(chips):
    return [[2 * chip + core for chip in CHIPS] for core in range(2)]


def shards(features, short_taps, long_filter, skip_gain, out_weight):
    chan = lax.axis_size("chan")
    chips = chan // 2
    groups = gather_groups(chips)
    sent = gated_copies(features, short_taps, long_filter, skip_gain, chips)
    own = lax.all_to_all(sent, "chan", 0, 0, tiled=True, axis_index_groups=groups)
    other = lax.ppermute(own, "chan", [(d, d ^ 1) for d in range(chan)])
    blocks = out_weight.reshape(chan, 4, N2)
    sides = [jnp.concatenate([blocks[d] for d in groups[g] + groups[1 - g]], axis=0) for g in range(2)]
    weight = jnp.where(lax.axis_index("chan") % 2 == 0, sides[0], sides[1])
    return pl.pallas_call(
        project_kernel,
        out_shape=jax.ShapeDtypeStruct((BLOCK, N2), bf16),
        in_specs=[vmem] * 3,
        out_specs=hbm,
        scratch_shapes=[pltpu.VMEM((BLOCK, N2), bf16), pltpu.SemaphoreType.DMA((8,))],
        compiler_params=pltpu.CompilerParams(vmem_limit_bytes=24 << 20),
        cost_estimate=pl.CostEstimate(flops=1 << 28, bytes_accessed=1 << 22, transcendentals=0),
    )(own.reshape(4 * chips, BLOCK), other.reshape(chips, 4, N1, N2), weight)


def solution(mesh):
    placed = (
        P(None, "chan", "seq"),
        P(None, "chan", None),
        P("chan", "seq"),
        P("chan"),
        P(None, "chan"),
    )
    return jax.shard_map(
        shards, mesh=mesh, in_specs=placed, out_specs=P("seq", "chan"), check_vma=False
    )
```
